32 devices in a mesh: chan: 2 (over x), tm: 16 (over z, y, core).
Axes of the slice: x: 2, y: 2, z: 4, core: 2. Of those that a mesh axis runs over, the one named last changes fastest.
Arguments:
- voltages: bfloat16 [8, 2, 128, 32768], P(None, None, 'chan', 'tm'), may hold values from -100 to 100
- prototype: float32 [64], replicated, may hold values from -5 to 5
- forget: float32 [8], P('chan'), may hold values from 0.5 to 16
Outputs:
- whitened: bfloat16 [8, 256, 32768], P('chan', None, 'tm')
The draws below stay inside these ranges and needn't reach their ends.
All inputs are finite; a program needn't handle non-finite values.
Results may differ from the reference program's by a relative error of at most 0.0071.
Values may be sent and summed in bfloat16 or wider, within the bound.
A program may use at most 128 MiB of HBM per device.

```python
import math
import jax
import jax.numpy as jnp
from jax import lax

CHANNELS = 8
TAPS = 8
ANTENNAS = 128
SNAP_DEV = 2048
FRAMES = 32768
N_TM = 16


def draw_voltages(key, part):
    keys = jax.random.split(key, 7)
    array_shape = (CHANNELS, 2, ANTENNAS, FRAMES)
    gains = jnp.exp(jax.random.uniform(keys[0], (1, 2, ANTENNAS, 1), jnp.float32, 0.0, 2.302585))
    noise = jax.random.normal(keys[1], array_shape, jnp.float32)
    strength = 0.6
    source_one = jax.random.normal(keys[2], (CHANNELS, 2, 1, FRAMES), jnp.float32)
    source_two = jax.random.normal(keys[3], (CHANNELS, 2, 1, FRAMES), jnp.float32)
    weight_one = jax.random.normal(keys[4], (1, 2, ANTENNAS, 1), jnp.float32)
    weight_two = jax.random.normal(keys[5], (1, 2, ANTENNAS, 1), jnp.float32)
    segment = SNAP_DEV // 4
    envelope = jnp.exp(jax.random.uniform(keys[6], (1, 1, 1, FRAMES // segment), jnp.float32, -1.0, 1.0))
    envelope = jnp.repeat(envelope, segment, axis=3)
    signal = noise + strength * (weight_one * source_one + weight_two * source_two)
    return jnp.clip(envelope * gains * signal, -100.0, 100.0).astype(jnp.bfloat16)


def shard_levels(rng, shape, cuts, smallest, high):
    def one(axis_at, blocks):
        steps = jax.random.uniform(jax.random.fold_in(jax.random.fold_in(rng, 6), axis_at), (blocks,), jnp.float32, smallest / len(cuts), high / len(cuts))
        return jnp.repeat(jnp.exp(steps), shape[axis_at] // blocks).reshape((-1,) + (1,) * (len(shape) - axis_at - 1))

    level = one(*cuts[0])
    for cut in cuts[1:]:
        level = level * one(*cut)
    return level


def bell_draw(rng, dims, scale, limit, held_as=jnp.bfloat16):
    drawn = scale * jax.random.normal(rng, dims, jnp.float32)
    return jnp.clip(drawn, min=-limit, max=limit).astype(held_as)


def setup_inputs(seed: int = 0) -> dict:
    streams_of = jax.random.split(jax.random.key(seed), 4)
    return {
        "voltages": draw_voltages(jax.random.fold_in(streams_of[3], 71), 0),
        "prototype": bell_draw(streams_of[1], (TAPS * CHANNELS,), 0.35, 5.0, jnp.float32),
        "forget": jnp.clip(jnp.exp(math.log(16.0) - 3.465736 * jax.random.uniform(streams_of[2], (CHANNELS,), jnp.float32) ** shard_levels(streams_of[2], (CHANNELS,), ((0, 2),), -0.2, 0.2)), 0.5, 16.0),
    }


def coefficient_table(prototype, tap_count, filter_branches):
    shaped = prototype.reshape(tap_count, filter_branches)
    steps_p = jnp.arange(filter_branches, dtype=jnp.float32)
    phase = 2.0 * math.pi / filter_branches * (steps_p[:, None] * steps_p[None, :])
    cosine = jnp.cos(phase)
    sine = jnp.sin(phase)
    pattern = jnp.stack([jnp.stack([cosine, -sine], -1), jnp.stack([sine, cosine], -1)], axis=1)
    return (shaped[:, :, None, None, None] * pattern[None]).astype(jnp.bfloat16)

def reference(voltages, prototype, forget):
    coef_table = coefficient_table(prototype, TAPS, CHANNELS)
    retain = jnp.exp(-forget / N_TM)
    col_count = 2 * ANTENNAS
    identity_m = jnp.eye(col_count, dtype=jnp.float32)

    def block_step(carry, block_idx):
        tail_rows, prior_gram, prior_count = carry
        start = (block_idx * SNAP_DEV).astype(jnp.int32)
        block = lax.dynamic_slice_in_dim(voltages, start, SNAP_DEV, axis=3)
        extended = jnp.concatenate([tail_rows, block], axis=3).astype(jnp.float32)
        branch_sum = jnp.zeros((CHANNELS, ANTENNAS, 2, SNAP_DEV), jnp.float32)
        for tap_idx in range(TAPS):
            branch_sum = branch_sum + jnp.einsum('pcaf,pckq->kaqf', extended[..., tap_idx:tap_idx + SNAP_DEV], coef_table[tap_idx].astype(jnp.float32))
        spectrum_rows = branch_sum.reshape(CHANNELS, col_count, SNAP_DEV).astype(jnp.bfloat16)
        spec_f = spectrum_rows.astype(jnp.float32)
        gram_now = jnp.einsum('cif,cjf->cij', spec_f, spec_f)
        moment = retain[:, None, None] * prior_gram + gram_now
        weight_sum = retain * prior_count + jnp.float32(SNAP_DEV)
        factor_low = jnp.linalg.cholesky(moment / weight_sum[:, None, None])
        inverse = lax.linalg.triangular_solve(factor_low, jnp.broadcast_to(identity_m, factor_low.shape), left_side=True, lower=True)
        whitened = jnp.einsum('cij,cjf->cif', inverse, spec_f, precision=lax.Precision.HIGHEST).astype(jnp.bfloat16)
        new_tail = block[..., SNAP_DEV - (TAPS - 1):]
        return ((new_tail, moment, weight_sum), whitened)
    init = (jnp.zeros((CHANNELS, 2, ANTENNAS, TAPS - 1), jnp.bfloat16), jnp.zeros((CHANNELS, col_count, col_count), jnp.float32), jnp.zeros((CHANNELS,), jnp.float32))
    _, block_list = lax.scan(block_step, init, jnp.arange(N_TM, dtype=jnp.int32))
    return jnp.transpose(block_list, (1, 2, 0, 3)).reshape(CHANNELS, col_count, N_TM * SNAP_DEV)
```

```python
import math

import jax
import jax.numpy as jnp
from jax import lax
from jax.experimental import pallas as pl
from jax.experimental.pallas import tpu as pltpu
from jax.sharding import PartitionSpec as P


GROUP = 8
BASE = 128


def passed_along(value, axis, steps):
    count = lax.axis_size(axis)
    leading, last = (max(0, -steps), min(count, count - steps))
    return lax.ppermute(value, axis, [(source, source + steps) for source in range(leading, last)])


def carried_in(value, axis, join, neutral):
    count, mine = (lax.axis_size(axis), lax.axis_index(axis))
    pieces = jax.tree.map(lambda part: lax.all_gather(part, axis), value)
    total = jax.tree.map(
        lambda part, zero: jnp.full_like(part, 0) + jnp.asarray(zero, part.dtype), value, neutral
    )

    def hop(position, total):
        longer = join(total, jax.tree.map(lambda part: part[position], pieces))
        return jax.tree.map(lambda new, old: jnp.where(position < mine, new, old), longer, total)

    return lax.fori_loop(0, count - 1, hop, total)


def coefficient_table(prototype, tap_count, filter_branches):
    shaped = prototype.reshape(tap_count, filter_branches)
    steps_p = jnp.arange(filter_branches, dtype=jnp.float32)
    phase = 2.0 * math.pi / filter_branches * (steps_p[:, None] * steps_p[None, :])
    cosine = jnp.cos(phase)
    sine = jnp.sin(phase)
    pattern = jnp.stack([jnp.stack([cosine, -sine], -1), jnp.stack([sine, cosine], -1)], axis=1)
    return (shaped[:, :, None, None, None] * pattern[None]).astype(jnp.bfloat16)


def combine_stats(earlier, later):
    gram_e, count_e, retain_e = earlier
    gram_l, count_l, retain_l = later
    return (
        gram_e * retain_l[:, None, None] + gram_l,
        count_e * retain_l + count_l,
        retain_e * retain_l,
    )


def per_device(voltages, prototype, forget):
    filter_branches = voltages.shape[0]
    local_antenna_count = voltages.shape[2]
    frame_rows = voltages.shape[3]
    tap_count = prototype.shape[0] // filter_branches
    coef_table = coefficient_table(prototype, tap_count, filter_branches)
    tail_rows = passed_along(voltages[..., frame_rows - (tap_count - 1) :], "tm", 1)
    extended = jnp.concatenate([tail_rows, voltages], axis=3)
    branch_sum = jnp.zeros((filter_branches, local_antenna_count, 2, frame_rows), jnp.float32)
    for tap_idx in range(tap_count):
        branch_sum = branch_sum + jnp.einsum(
            "pcaf,pckq->kaqf",
            extended[..., tap_idx : tap_idx + frame_rows],
            coef_table[tap_idx],
            preferred_element_type=jnp.float32,
        )
    spectrum_rows = branch_sum.reshape(filter_branches, local_antenna_count * 2, frame_rows).astype(
        jnp.bfloat16
    )
    turned = lax.all_to_all(spectrum_rows, "chan", split_axis=0, concat_axis=1, tiled=True)
    channels_per_device = turned.shape[0]
    col_count = turned.shape[1]
    gram_now = jnp.einsum("cif,cjf->cij", turned, turned, preferred_element_type=jnp.float32)
    retain = jnp.exp(-forget / lax.axis_size("tm"))
    row_count = jnp.full((channels_per_device,), float(frame_rows), jnp.float32)
    zero_count = jnp.zeros((channels_per_device,), jnp.float32)
    unit_retain = jnp.ones((channels_per_device,), jnp.float32)
    prior_gram, prior_count, unused_retain = carried_in(
        (gram_now, row_count, retain),
        "tm",
        combine_stats,
        (jnp.zeros_like(gram_now), zero_count, unit_retain),
    )
    moment = retain[:, None, None] * prior_gram + gram_now
    weight_sum = retain * prior_count + jnp.float32(frame_rows)
    scaled = moment / weight_sum[:, None, None]
    half = col_count // 2
    blocks = jnp.stack(
        [scaled[:, :half, :half], scaled[:, half:, :half], scaled[:, half:, half:]], axis=1
    )
    return whitened_by(blocks, turned)


def split3(x):
    high = x.astype(jnp.bfloat16)
    rest = x - high.astype(jnp.float32)
    mid = rest.astype(jnp.bfloat16)
    low = (rest - mid.astype(jnp.float32)).astype(jnp.bfloat16)
    return high, mid, low


def exact_dot(a, b, dims):
    return lax.dot_general(
        a, b, (dims, ((), ())), precision=lax.Precision.HIGHEST, preferred_element_type=jnp.float32
    )


def eliminate(work, done, channels):
    lane = lax.broadcasted_iota(jnp.int32, (GROUP, BASE), 1)
    row = lax.broadcasted_iota(jnp.int32, (GROUP, BASE), 0)

    def group_step(group, _):
        first = pl.multiple_of(group * GROUP, GROUP)
        trailing = lane < BASE - first
        panels, columns, scales = [], [], []
        for c in range(channels):
            panel = work[c, pl.ds(first, GROUP), :]
            columns.append(
                [jnp.broadcast_to(panel[:, q : q + 1], (GROUP, BASE)) for q in range(GROUP)]
            )
            panels.append(jnp.where(lane < GROUP, (lane == row).astype(jnp.float32), panel))
            scales.append(jnp.zeros((GROUP, BASE), jnp.float32))
        for p in range(GROUP):
            for c in range(channels):
                column = columns[c]
                pivot = jnp.broadcast_to(column[p][p : p + 1, :], (GROUP, BASE))
                inverse = 1.0 / pivot
                scales[c] = jnp.where(row == p, inverse, scales[c])
                if p + 1 < GROUP:
                    factor = jnp.where(row > p, column[p] * inverse, 0.0)
                    for q in range(p + 1, GROUP):
                        column[q] = column[q] - factor * column[q][p : p + 1, :]
                    panels[c] = panels[c] - factor * panels[c][p : p + 1, :]
        for c in range(channels):
            panel = panels[c]
            scaled = panel * scales[c]
            final = jnp.where(trailing & (lane >= GROUP), 0.0, panel) * jnp.sqrt(scales[c])
            done[c, pl.ds(first, GROUP), :] = pltpu.roll(final, first, 1)
            left = pltpu.roll(jnp.where(trailing & (lane >= GROUP), panel, 0.0), first, 1)
            lh, lm, ll = split3(left)
            rh, rm, rl = split3(scaled)
            lefts = jnp.concatenate([lh, lh, lh, lm, lm, ll], 0)
            rights = jnp.concatenate([rh, rm, rl, rh, rm, rh], 0)
            update = lax.dot_general(
                lefts, rights, (((0,), (0,)), ((), ())), preferred_element_type=jnp.float32
            )
            wide = lax.broadcasted_iota(jnp.int32, (BASE, BASE), 1)
            kept = jnp.where(wide < GROUP, 0.0, work[c])
            work[c] = pltpu.roll(kept - update, BASE - GROUP, 1)
        return 0

    lax.fori_loop(0, BASE // GROUP, group_step, 0)


def whiten_kernel(moment_ref, x_ref, out_ref, work, done, low21, high, low):
    channels = moment_ref.shape[0]
    step = pl.program_id(0)

    @pl.when(step == 0)
    def _():
        for c in range(channels):
            work[c] = moment_ref[c, 0]
        eliminate(work, done, channels)
        for c in range(channels):
            inverse = done[c]
            factor = exact_dot(moment_ref[c, 1], inverse, ((1,), (1,)))
            work[c] = moment_ref[c, 2] - exact_dot(factor, factor, ((1,), (1,)))
            low21[c] = exact_dot(factor, inverse, ((1,), (0,)))
            first = inverse.astype(jnp.bfloat16)
            high[c, :BASE, :BASE] = first
            low[c, :BASE, :BASE] = (inverse - first.astype(jnp.float32)).astype(jnp.bfloat16)
            high[c, :BASE, BASE:] = jnp.zeros((BASE, BASE), jnp.bfloat16)
            low[c, :BASE, BASE:] = jnp.zeros((BASE, BASE), jnp.bfloat16)
        eliminate(work, done, channels)
        for c in range(channels):
            inverse = done[c]
            corner = -exact_dot(inverse, low21[c], ((1,), (0,)))
            for at, part in ((0, corner), (BASE, inverse)):
                first = part.astype(jnp.bfloat16)
                high[c, BASE:, at : at + BASE] = first
                low[c, BASE:, at : at + BASE] = (part - first.astype(jnp.float32)).astype(
                    jnp.bfloat16
                )

    x = x_ref[0]
    total = jnp.dot(high[step], x, preferred_element_type=jnp.float32)
    total += jnp.dot(low[step], x, preferred_element_type=jnp.float32)
    out_ref[0] = total.astype(jnp.bfloat16)


def whitened_by(moment, spectra):
    channels, rows, frames = spectra.shape
    square = (channels, BASE, BASE)
    return pl.pallas_call(
        whiten_kernel,
        grid=(channels,),
        out_shape=jax.ShapeDtypeStruct(spectra.shape, jnp.bfloat16),
        in_specs=[
            pl.BlockSpec((channels, 3, BASE, BASE), lambda c: (0, 0, 0, 0)),
            pl.BlockSpec((1, rows, frames), lambda c: (c, 0, 0)),
        ],
        out_specs=pl.BlockSpec((1, rows, frames), lambda c: (c, 0, 0)),
        scratch_shapes=[
            pltpu.VMEM(square, jnp.float32),
            pltpu.VMEM(square, jnp.float32),
            pltpu.VMEM(square, jnp.float32),
            pltpu.VMEM((channels, rows, rows), jnp.bfloat16),
            pltpu.VMEM((channels, rows, rows), jnp.bfloat16),
        ],
        compiler_params=pltpu.CompilerParams(vmem_limit_bytes=40 << 20),
        name="whiten",
    )(moment, spectra)


def solution(mesh):
    placed = (P(None, None, "chan", "tm"), P(), P("chan"))
    return jax.shard_map(
        per_device, mesh=mesh, in_specs=placed, out_specs=P("chan", None, "tm"), check_vma=False
    )
```

```python
import functools
import math

import jax
import jax.numpy as jnp
from jax import lax
from jax.experimental import pallas as pl
from jax.experimental.pallas import tpu as pltpu
from jax.sharding import PartitionSpec as P

GROUP = 8
BASE = 128


def split3(x):
    high = x.astype(jnp.bfloat16)
    rest = x - high.astype(jnp.float32)
    mid = rest.astype(jnp.bfloat16)
    low = (rest - mid.astype(jnp.float32)).astype(jnp.bfloat16)
    return high, mid, low


def exact_dot(a, b, dims):
    return lax.dot_general(
        a, b, (dims, ((), ())), precision=lax.Precision.HIGHEST, preferred_element_type=jnp.float32
    )


def eliminate(work, done, channels):
    lane = lax.broadcasted_iota(jnp.int32, (GROUP, BASE), 1)
    row = lax.broadcasted_iota(jnp.int32, (GROUP, BASE), 0)

    def group_step(group, _):
        first = pl.multiple_of(group * GROUP, GROUP)
        trailing = lane < BASE - first
        panels, columns, scales = [], [], []
        for c in range(channels):
            panel = work[c, pl.ds(first, GROUP), :]
            columns.append(
                [jnp.broadcast_to(panel[:, q : q + 1], (GROUP, BASE)) for q in range(GROUP)]
            )
            panels.append(jnp.where(lane < GROUP, (lane == row).astype(jnp.float32), panel))
            scales.append(jnp.zeros((GROUP, BASE), jnp.float32))
        for p in range(GROUP):
            for c in range(channels):
                column = columns[c]
                pivot = jnp.broadcast_to(column[p][p : p + 1, :], (GROUP, BASE))
                inverse = 1.0 / pivot
                scales[c] = jnp.where(row == p, inverse, scales[c])
                if p + 1 < GROUP:
                    factor = jnp.where(row > p, column[p] * inverse, 0.0)
                    for q in range(p + 1, GROUP):
                        column[q] = column[q] - factor * column[q][p : p + 1, :]
                    panels[c] = panels[c] - factor * panels[c][p : p + 1, :]
        for c in range(channels):
            panel = panels[c]
            scaled = panel * scales[c]
            final = jnp.where(trailing & (lane >= GROUP), 0.0, panel) * jnp.sqrt(scales[c])
            done[c, pl.ds(first, GROUP), :] = pltpu.roll(final, first, 1)
            left = pltpu.roll(jnp.where(trailing & (lane >= GROUP), panel, 0.0), first, 1)
            lh, lm, ll = split3(left)
            rh, rm, rl = split3(scaled)
            lefts = jnp.concatenate([lh, lh, lh, lm, lm, ll], 0)
            rights = jnp.concatenate([rh, rm, rl, rh, rm, rh], 0)
            update = lax.dot_general(
                lefts, rights, (((0,), (0,)), ((), ())), preferred_element_type=jnp.float32
            )
            wide = lax.broadcasted_iota(jnp.int32, (BASE, BASE), 1)
            kept = jnp.where(wide < GROUP, 0.0, work[c])
            work[c] = pltpu.roll(kept - update, BASE - GROUP, 1)
        return 0

    lax.fori_loop(0, BASE // GROUP, group_step, 0)


def whiten_kernel(moment_ref, x_ref, out_ref, work, done, low21, high, low):
    channels = moment_ref.shape[0]
    step = pl.program_id(0)

    @pl.when(step == 0)
    def _():
        for c in range(channels):
            work[c] = moment_ref[c, 0]
        eliminate(work, done, channels)
        for c in range(channels):
            inverse = done[c]
            factor = exact_dot(moment_ref[c, 1], inverse, ((1,), (1,)))
            work[c] = moment_ref[c, 2] - exact_dot(factor, factor, ((1,), (1,)))
            low21[c] = exact_dot(factor, inverse, ((1,), (0,)))
            first = inverse.astype(jnp.bfloat16)
            high[c, :BASE, :BASE] = first
            low[c, :BASE, :BASE] = (inverse - first.astype(jnp.float32)).astype(jnp.bfloat16)
            high[c, :BASE, BASE:] = jnp.zeros((BASE, BASE), jnp.bfloat16)
            low[c, :BASE, BASE:] = jnp.zeros((BASE, BASE), jnp.bfloat16)
        eliminate(work, done, channels)
        for c in range(channels):
            inverse = done[c]
            corner = -exact_dot(inverse, low21[c], ((1,), (0,)))
            for at, part in ((0, corner), (BASE, inverse)):
                first = part.astype(jnp.bfloat16)
                high[c, BASE:, at : at + BASE] = first
                low[c, BASE:, at : at + BASE] = (part - first.astype(jnp.float32)).astype(
                    jnp.bfloat16
                )

    x = x_ref[0]
    total = jnp.dot(high[step], x, preferred_element_type=jnp.float32)
    total += jnp.dot(low[step], x, preferred_element_type=jnp.float32)
    out_ref[0] = total.astype(jnp.bfloat16)


def whitened_by(moment, spectra):
    channels, rows, frames = spectra.shape
    square = (channels, BASE, BASE)
    return pl.pallas_call(
        whiten_kernel,
        grid=(channels,),
        out_shape=jax.ShapeDtypeStruct(spectra.shape, jnp.bfloat16),
        in_specs=[
            pl.BlockSpec((channels, 3, BASE, BASE), lambda c: (0, 0, 0, 0)),
            pl.BlockSpec((1, rows, frames), lambda c: (c, 0, 0)),
        ],
        out_specs=pl.BlockSpec((1, rows, frames), lambda c: (c, 0, 0)),
        scratch_shapes=[
            pltpu.VMEM(square, jnp.float32),
            pltpu.VMEM(square, jnp.float32),
            pltpu.VMEM(square, jnp.float32),
            pltpu.VMEM((channels, rows, rows), jnp.bfloat16),
            pltpu.VMEM((channels, rows, rows), jnp.bfloat16),
        ],
        compiler_params=pltpu.CompilerParams(vmem_limit_bytes=40 << 20),
        name="whiten",
    )(moment, spectra)


PLANE = 4
PIECE = 16
HALO = 128
TILE = 512


def digits(shape, axis, unit, count):
    return (lax.broadcasted_iota(jnp.int32, shape, axis) // unit) % count


def turn_kernel(
    taps, chan_count, tm_count,
    volts, coef, retain, inverse_weight,
    spectra, moment,
    extended, table, outgoing, gram, plane_in, chain_in, chain_out, plane_out,
    load_sem, halo_send, halo_recv, turn_send, turn_recv,
    spread_send, spread_recv, chain_send, chain_recv, back_send, back_recv,
):
    inputs, antennas, frames = volts.shape
    channels = spectra.shape[0]
    pieces = antennas // PIECE
    piece_rows = 2 * PIECE
    quarter = moment.shape[1] // PLANE
    chan, tm = lax.axis_index("chan"), lax.axis_index("tm")
    plane, spot = tm // PLANE, tm % PLANE
    plane_count = tm_count // PLANE

    def remote(src, dst, send, recv, chan_to, tm_to):
        return pltpu.make_async_remote_copy(
            src_ref=src, dst_ref=dst, send_sem=send, recv_sem=recv,
            device_id=(chan_to, tm_to), device_id_type=pl.DeviceIdType.MESH,
        )

    def mate(step):
        return plane * PLANE + (spot + step) % PLANE

    loads = []
    for g in range(pieces):
        rows = pl.ds(g * PIECE, PIECE)
        loads.append(
            pltpu.make_async_copy(
                volts.at[:, rows, :], extended.at[:, rows, pl.ds(HALO, frames)], load_sem.at[g]
            )
        )
        loads[-1].start()

    barrier = pltpu.get_barrier_semaphore()

    def greet(chan_to, tm_to):
        pl.semaphore_signal(
            barrier, inc=1, device_id=(chan_to, tm_to), device_id_type=pl.DeviceIdType.MESH
        )

    for s in range(1, chan_count):
        greet((chan + s) % chan_count, tm)
    for m in range(1, PLANE):
        greet(chan, mate(m))
    above, below = plane + 1 < plane_count, plane > 0
    peers = chan_count - 1 + PLANE - 1
    for step, reached in (
        (PLANE, above), (-PLANE, below), (1, above & (spot == PLANE - 1)), (-1, below & (spot == 0))
    ):
        peers = peers + jnp.where(reached, 1, 0)

        @pl.when(reached)
        def _():
            greet(chan, tm + step)

    rows, columns = table.shape
    kinds, terms = coef.shape
    pick_row = digits((rows, kinds), 0, piece_rows, rows // piece_rows) * 2 + digits((rows, kinds), 0, 1, 2)
    pick_row = pick_row == lax.broadcasted_iota(jnp.int32, (rows, kinds), 1)
    pick_column = digits((terms, columns), 1, PIECE, terms)
    pick_column = pick_column == lax.broadcasted_iota(jnp.int32, (terms, columns), 0)
    spread = jnp.dot(
        pick_row.astype(jnp.float32).astype(jnp.bfloat16), coef[...], preferred_element_type=jnp.float32
    ).astype(jnp.bfloat16)
    spread = jnp.dot(
        spread, pick_column.astype(jnp.float32).astype(jnp.bfloat16), preferred_element_type=jnp.float32
    )
    own = digits((rows, columns), 0, 2, PIECE) == digits((rows, columns), 1, 1, PIECE)
    table[...] = jnp.where(own, spread, 0.0).astype(jnp.bfloat16)

    pl.semaphore_wait(barrier, peers)

    tail = remote(
        volts.at[:, :, pl.ds(frames - HALO, HALO)], extended.at[:, :, pl.ds(0, HALO)],
        halo_send, halo_recv, chan, tm + 1,
    )

    @pl.when(tm + 1 < tm_count)
    def _():
        tail.start()

    @pl.when(tm == 0)
    def _():
        extended[:, :, :HALO] = jnp.zeros((inputs, antennas, HALO), jnp.bfloat16)

    @pl.when(tm > 0)
    def _():
        tail.wait_recv()

    base = chan * (2 * antennas)
    turns = {}

    def send_rows(s, c, g, start, count):
        turns[s, c, g] = remote(
            outgoing.at[s - 1, c, pl.ds(start, count), :],
            spectra.at[c, pl.ds(pl.multiple_of(base + start, piece_rows), count), :],
            turn_send.at[s - 1, c, g], turn_recv.at[s - 1, c, g],
            (chan + s) % chan_count, tm,
        )
        turns[s, c, g].start()

    for g in range(pieces):
        loads[g].wait()

        def tile(t, _):
            first = pl.multiple_of(t * TILE, TILE)
            block = extended[:, g * PIECE : (g + 1) * PIECE, pl.ds(first, TILE + HALO)]
            block = block.reshape(inputs * PIECE, TILE + HALO)
            shifted = [
                (pltpu.roll(block, taps - 1 - j, 1) if j < taps - 1 else block)[:, HALO:]
                for j in range(taps)
            ]
            result = jnp.dot(
                table[...], jnp.concatenate(shifted, 0), preferred_element_type=jnp.float32
            ).astype(jnp.bfloat16)
            for s in range(chan_count):
                for c in range(channels):
                    at = (s * channels + c) * piece_rows
                    part = result[at : at + piece_rows]
                    if s == 0:
                        start = pl.multiple_of(base + g * piece_rows, piece_rows)
                        spectra[c, pl.ds(start, piece_rows), pl.ds(first, TILE)] = part
                    else:
                        outgoing[s - 1, c, g * piece_rows : (g + 1) * piece_rows, pl.ds(first, TILE)] = part
            return 0

        lax.fori_loop(0, frames // TILE, tile, 0)
        for s in range(1, chan_count):
            send_rows(s, 0, g, g * piece_rows, piece_rows)
    for c in range(1, channels):
        for s in range(1, chan_count):
            send_rows(s, c, 0, 0, pieces * piece_rows)

    spreads, chains, backs = {}, {}, {}
    half = 2 * antennas * chan_count // 2

    def part_of(index):
        return pl.ds(pl.multiple_of(index * quarter, 8), quarter)

    def own_block(c):
        for key, copy in turns.items():
            if key[1] == c:
                copy.wait_recv()
        x = spectra[c]
        product = lax.dot_general(
            x, x, (((1,), (1,)), ((), ())), preferred_element_type=jnp.float32
        )
        gram[c, :half] = product[:half, :half]
        gram[c, half : 2 * half] = product[half:, :half]
        gram[c, 2 * half :] = product[half:, half:]
        for m in range(1, PLANE):
            spreads[c, m] = remote(
                gram.at[c, part_of((spot + m) % PLANE), :], plane_in.at[c, spot],
                spread_send.at[c, m - 1], spread_recv.at[c, m - 1], chan, mate(m),
            )
            spreads[c, m].start()
        plane_in[c, spot] = gram[c, part_of(spot), :]

    def carry(c):
        for m in range(1, PLANE):
            spreads[c, m].wait_recv()
        keep = retain[c]
        total = plane_in[c, 0]
        for i in range(1, PLANE):
            total = total * keep + plane_in[c, i]
        chains[c] = remote(
            chain_out.at[c], chain_in.at[c], chain_send.at[c], chain_recv.at[c], chan, tm + PLANE
        )

        @pl.when(plane == 0)
        def _():
            chain_in[c] = jnp.zeros_like(total)

        @pl.when(plane > 0)
        def _():
            chains[c].wait_recv()

        running = chain_in[c]
        square = keep * keep
        chain_out[c] = running * (square * square) + total

        @pl.when(plane + 1 < plane_count)
        def _():
            chains[c].start()

        for i in range(PLANE):
            running = running * keep + plane_in[c, i]
            plane_out[c, i] = running * inverse_weight[c, i]
        for m in range(1, PLANE):
            backs[c, m] = remote(
                plane_out.at[c, (spot + m) % PLANE], moment.at[c, part_of(spot), :],
                back_send.at[c, m - 1], back_recv.at[c, m - 1], chan, mate(m),
            )
            backs[c, m].start()
        moment[c, part_of(spot), :] = plane_out[c, spot]

    for c in range(channels):
        own_block(c)
        if c > 0:
            carry(c - 1)
    carry(channels - 1)

    for copy in backs.values():
        copy.wait()
    for copy in spreads.values():
        copy.wait_send()
    for copy in turns.values():
        copy.wait_send()

    @pl.when(plane + 1 < plane_count)
    def _():
        for copy in chains.values():
            copy.wait_send()

    @pl.when(tm + 1 < tm_count)
    def _():
        tail.wait_send()


def turned_and_carried(volts, coef, retain, inverse_weight, taps):
    inputs, antennas, frames = volts.shape
    channels = retain.shape[0]
    chan_count, tm_count = lax.axis_size("chan"), lax.axis_size("tm")
    columns = 2 * antennas * chan_count
    half = columns // 2
    quarter = 3 * half // PLANE
    rows = coef.shape[0] * PIECE
    pieces = antennas // PIECE
    dma = pltpu.SemaphoreType.DMA
    turn_shape = (chan_count - 1, channels, pieces)
    plane_shape = (channels, PLANE - 1)
    return pl.pallas_call(
        functools.partial(turn_kernel, taps, chan_count, tm_count),
        out_shape=(
            jax.ShapeDtypeStruct((channels, columns, frames), jnp.bfloat16),
            jax.ShapeDtypeStruct((channels, 3 * half, half), jnp.float32),
        ),
        in_specs=[
            pl.BlockSpec(memory_space=pl.ANY),
            pl.BlockSpec(memory_space=pltpu.VMEM),
            pl.BlockSpec(memory_space=pltpu.SMEM),
            pl.BlockSpec(memory_space=pltpu.SMEM),
        ],
        out_specs=(pl.BlockSpec(memory_space=pltpu.VMEM), pl.BlockSpec(memory_space=pltpu.VMEM)),
        scratch_shapes=[
            pltpu.VMEM((inputs, antennas, HALO + frames), jnp.bfloat16),
            pltpu.VMEM((rows, taps * inputs * PIECE), jnp.bfloat16),
            pltpu.VMEM((chan_count - 1, channels, 2 * antennas, frames), jnp.bfloat16),
            pltpu.VMEM((channels, 3 * half, half), jnp.float32),
            pltpu.VMEM((channels, PLANE, quarter, half), jnp.float32),
            pltpu.VMEM((channels, quarter, half), jnp.float32),
            pltpu.VMEM((channels, quarter, half), jnp.float32),
            pltpu.VMEM((channels, PLANE, quarter, half), jnp.float32),
            dma((pieces,)), dma, dma, dma(turn_shape), dma(turn_shape),
            dma(plane_shape), dma(plane_shape), dma((channels,)), dma((channels,)),
            dma(plane_shape), dma(plane_shape),
        ],
        compiler_params=pltpu.CompilerParams(
            collective_id=0, has_side_effects=True, vmem_limit_bytes=40 << 20
        ),
        name="turn",
    )(volts, coef, retain, inverse_weight)


def coefficient_rows(prototype, tap_count, branches, first):
    shaped = prototype.reshape(tap_count, branches)
    steps_p = jnp.arange(branches, dtype=jnp.float32)
    steps_k = ((jnp.arange(branches) + first) % branches).astype(jnp.float32)
    phase = 2.0 * math.pi / branches * (steps_k[:, None] * steps_p[None, :])
    cosine, sine = jnp.cos(phase), jnp.sin(phase)
    pattern = jnp.stack([jnp.stack([cosine, sine], -1), jnp.stack([-sine, cosine], -1)], axis=1)
    table = shaped[None, None, :, :, None] * pattern[:, :, None, :, :]
    return table.astype(jnp.bfloat16).reshape(2 * branches, tap_count * branches * 2)


def per_device(voltages, prototype, forget):
    branches, parts, antennas, frames = voltages.shape
    taps = prototype.shape[0] // branches
    channels = forget.shape[0]
    tm_count = lax.axis_size("tm")
    coef = coefficient_rows(prototype, taps, branches, lax.axis_index("chan") * channels)
    rate = -forget / tm_count
    ages = jnp.arange(tm_count)
    spots = lax.axis_index("tm") // PLANE * PLANE + jnp.arange(PLANE)
    held = jnp.where(ages <= spots[:, None], 1.0, 0.0)
    powers = jnp.exp(rate[:, None] * ages.astype(jnp.float32))
    weight = frames * jnp.sum(powers[:, None, :] * held[None], -1)
    volts = voltages.reshape(branches * parts, antennas, frames)
    spectra, moment = turned_and_carried(volts, coef, jnp.exp(rate), 1.0 / weight, taps)
    return whitened_by(moment.reshape(channels, 3, BASE, BASE), spectra)


def solution(mesh):
    placed = (P(None, None, "chan", "tm"), P(), P("chan"))
    return jax.shard_map(
        per_device, mesh=mesh, in_specs=placed, out_specs=P("chan", None, "tm"), check_vma=False
    )
```

```python
import functools
import math

import jax
import jax.numpy as jnp
import numpy as np
from jax import lax
from jax.experimental import pallas as pl
from jax.experimental.pallas import tpu as pltpu
from jax.sharding import PartitionSpec as P

GROUP = 16
SUB = 8
BASE = 128


def split3(x):
    high = x.astype(jnp.bfloat16)
    rest = x - high.astype(jnp.float32)
    mid = rest.astype(jnp.bfloat16)
    low = (rest - mid.astype(jnp.float32)).astype(jnp.bfloat16)
    return high, mid, low


def exact_dot(a, b, dims):
    return lax.dot_general(
        a, b, (dims, ((), ())), precision=lax.Precision.HIGHEST, preferred_element_type=jnp.float32
    )


def eliminate(work, done, channels):
    lane = lax.broadcasted_iota(jnp.int32, (GROUP, BASE), 1)
    row = lax.broadcasted_iota(jnp.int32, (GROUP, BASE), 0)
    below = lax.broadcasted_iota(jnp.int32, (SUB, BASE), 0)
    subs = GROUP // SUB

    def group_step(group, _):
        first = pl.multiple_of(group * GROUP, GROUP)
        trailing = (lane < BASE - first) & (lane >= GROUP)
        panels, columns, scales = [], [], []
        for c in channels:
            panel = work[c, pl.ds(first, GROUP), :]
            columns.append([
                [
                    jnp.broadcast_to(panel[h * SUB : (h + 1) * SUB, q : q + 1], (SUB, BASE))
                    for h in range(subs)
                ]
                for q in range(GROUP)
            ])
            panel = jnp.where(lane < GROUP, (lane == row).astype(jnp.float32), panel)
            panels.append([panel[h * SUB : (h + 1) * SUB] for h in range(subs)])
            scales.append([jnp.zeros((SUB, BASE), jnp.float32) for h in range(subs)])
        for p in range(GROUP):
            at, inner = p // SUB, p % SUB
            for i in range(len(channels)):
                column = columns[i]
                pivot = jnp.broadcast_to(column[p][at][inner : inner + 1, :], (SUB, BASE))
                inverse = 1.0 / pivot
                scales[i][at] = jnp.where(below == inner, inverse, scales[i][at])
                for h in range(at, subs):
                    factor = column[p][h]
                    if h == at:
                        factor = jnp.where(below > inner, factor, 0.0)
                    factor = factor * inverse
                    for part in column[p + 1 :] + [panels[i]]:
                        if h == at:
                            continue
                        part[h] = part[h] - factor * part[at][inner : inner + 1, :]
                    if h == at:
                        own = factor
                for part in column[p + 1 :] + [panels[i]]:
                    part[at] = part[at] - own * part[at][inner : inner + 1, :]
        for i, c in enumerate(channels):
            panel = jnp.concatenate(panels[i], 0)
            scale = jnp.concatenate(scales[i], 0)
            left = pltpu.roll(jnp.where(trailing, panel, 0.0), first, 1)
            lh, lm, ll = split3(left)
            rh, rm, rl = split3(panel * scale)
            lefts = jnp.concatenate([lh, lh, lh, lm, lm, ll], 0)
            rights = jnp.concatenate([rh, rm, rl, rh, rm, rh], 0)
            update = lax.dot_general(
                lefts, rights, (((0,), (0,)), ((), ())), preferred_element_type=jnp.float32
            )
            wide = lax.broadcasted_iota(jnp.int32, (BASE, BASE), 1)
            kept = jnp.where(wide < GROUP, 0.0, work[c])
            work[c] = pltpu.roll(kept - update, BASE - GROUP, 1)
            final = jnp.where(trailing, 0.0, panel) * jnp.sqrt(scale)
            done[c, pl.ds(first, GROUP), :] = pltpu.roll(final, first, 1)
        return 0

    lax.fori_loop(0, BASE // GROUP, group_step, 0)


def whiten_kernel(moment_ref, x_ref, out_ref, work, done, low21, high, low):
    channels = moment_ref.shape[0]
    step = pl.program_id(0)

    @pl.when(step == 0)
    def _():
        for c in range(channels):
            work[c] = moment_ref[c, 0]
        eliminate(work, done, range(channels))
        for c in range(channels):
            inverse = done[c]
            factor = exact_dot(moment_ref[c, 1], inverse, ((1,), (1,)))
            work[c] = moment_ref[c, 2] - exact_dot(factor, factor, ((1,), (1,)))
            low21[c] = exact_dot(factor, inverse, ((1,), (0,)))
            first = inverse.astype(jnp.bfloat16)
            high[c, :BASE, :BASE] = first
            low[c, :BASE, :BASE] = (inverse - first.astype(jnp.float32)).astype(jnp.bfloat16)
            high[c, :BASE, BASE:] = jnp.zeros((BASE, BASE), jnp.bfloat16)
            low[c, :BASE, BASE:] = jnp.zeros((BASE, BASE), jnp.bfloat16)
        eliminate(work, done, range(channels))
        for c in range(channels):
            inverse = done[c]
            corner = -exact_dot(inverse, low21[c], ((1,), (0,)))
            for at, part in ((0, corner), (BASE, inverse)):
                first = part.astype(jnp.bfloat16)
                high[c, BASE:, at : at + BASE] = first
                low[c, BASE:, at : at + BASE] = (part - first.astype(jnp.float32)).astype(
                    jnp.bfloat16
                )

    x = x_ref[0]
    total = jnp.dot(high[step], x, preferred_element_type=jnp.float32)
    total += jnp.dot(low[step], x, preferred_element_type=jnp.float32)
    out_ref[0] = total.astype(jnp.bfloat16)


def whitened_by(moment, spectra):
    channels, rows, frames = spectra.shape
    square = (channels, BASE, BASE)
    return pl.pallas_call(
        whiten_kernel,
        grid=(channels,),
        out_shape=jax.ShapeDtypeStruct(spectra.shape, jnp.bfloat16),
        in_specs=[
            pl.BlockSpec((channels, 3, BASE, BASE), lambda c: (0, 0, 0, 0)),
            pl.BlockSpec((1, rows, frames), lambda c: (c, 0, 0)),
        ],
        out_specs=pl.BlockSpec((1, rows, frames), lambda c: (c, 0, 0)),
        scratch_shapes=[
            pltpu.VMEM(square, jnp.float32),
            pltpu.VMEM(square, jnp.float32),
            pltpu.VMEM(square, jnp.float32),
            pltpu.VMEM((channels, rows, rows), jnp.bfloat16),
            pltpu.VMEM((channels, rows, rows), jnp.bfloat16),
        ],
        compiler_params=pltpu.CompilerParams(vmem_limit_bytes=40 << 20),
        name="whiten",
    )(moment, spectra)


PLANE = 4
PIECE = 16
HALO = 128
TILE = 512


def digits(shape, axis, unit, count):
    return (lax.broadcasted_iota(jnp.int32, shape, axis) // unit) % count


def turn_kernel(
    taps, chan_count, tm_count,
    volts, coef, retain, inverse_weight,
    spectra, moment,
    extended, table, outgoing, gram, plane_in, chain_in, chain_out, plane_out,
    load_sem, halo_send, halo_recv, turn_send, turn_recv,
    spread_send, spread_recv, chain_send, chain_recv, back_send, back_recv,
):
    inputs, antennas, frames = volts.shape
    channels = spectra.shape[0]
    pieces = antennas // PIECE
    piece_rows = 2 * PIECE
    quarter = moment.shape[1] // PLANE
    chan, tm = lax.axis_index("chan"), lax.axis_index("tm")
    plane, spot = tm // PLANE, tm % PLANE
    plane_count = tm_count // PLANE
    rounds = chain_out.shape[1]

    def remote(src, dst, send, recv, chan_to, tm_to):
        return pltpu.make_async_remote_copy(
            src_ref=src, dst_ref=dst, send_sem=send, recv_sem=recv,
            device_id=(chan_to, tm_to), device_id_type=pl.DeviceIdType.MESH,
        )

    def mate(step):
        return plane * PLANE + (spot + step) % PLANE

    loads = []
    for g in range(pieces):
        rows = pl.ds(g * PIECE, PIECE)
        loads.append(
            pltpu.make_async_copy(
                volts.at[:, rows, :], extended.at[:, rows, pl.ds(HALO, frames)], load_sem.at[g]
            )
        )
        loads[-1].start()

    barrier = pltpu.get_barrier_semaphore()

    def greet(chan_to, tm_to):
        pl.semaphore_signal(
            barrier, inc=1, device_id=(chan_to, tm_to), device_id_type=pl.DeviceIdType.MESH
        )

    for s in range(1, chan_count):
        greet((chan + s) % chan_count, tm)
    for m in range(1, PLANE):
        greet(chan, mate(m))
    peers = chan_count - 1 + PLANE - 1
    hops = [PLANE**r * d for r in range(rounds) for d in range(1, PLANE)]
    meetings = [(PLANE * hop, plane + hop < plane_count) for hop in hops]
    meetings += [(-PLANE * hop, plane >= hop) for hop in hops]
    meetings.append((1, (plane + 1 < plane_count) & (spot == PLANE - 1)))
    meetings.append((-1, (plane > 0) & (spot == 0)))
    for step, reached in meetings:
        peers = peers + jnp.where(reached, 1, 0)

        @pl.when(reached)
        def _():
            greet(chan, tm + step)

    rows, columns = table.shape
    kinds, terms = coef.shape
    pick_row = digits((rows, kinds), 0, piece_rows, rows // piece_rows) * 2 + digits((rows, kinds), 0, 1, 2)
    pick_row = pick_row == lax.broadcasted_iota(jnp.int32, (rows, kinds), 1)
    pick_column = digits((terms, columns), 1, PIECE, terms)
    pick_column = pick_column == lax.broadcasted_iota(jnp.int32, (terms, columns), 0)
    spread = jnp.dot(
        pick_row.astype(jnp.float32).astype(jnp.bfloat16), coef[...], preferred_element_type=jnp.float32
    ).astype(jnp.bfloat16)
    spread = jnp.dot(
        spread, pick_column.astype(jnp.float32).astype(jnp.bfloat16), preferred_element_type=jnp.float32
    )
    own = digits((rows, columns), 0, 2, PIECE) == digits((rows, columns), 1, 1, PIECE)
    table[...] = jnp.where(own, spread, 0.0).astype(jnp.bfloat16)

    pl.semaphore_wait(barrier, peers)

    tails = []
    for g in range(pieces):
        rows = pl.ds(g * PIECE, PIECE)
        tails.append(
            remote(
                volts.at[:, rows, pl.ds(frames - HALO, HALO)], extended.at[:, rows, pl.ds(0, HALO)],
                halo_send.at[g], halo_recv.at[g], chan, tm + 1,
            )
        )

    @pl.when(tm + 1 < tm_count)
    def _():
        for tail in tails:
            tail.start()

    @pl.when(tm == 0)
    def _():
        extended[:, :, :HALO] = jnp.zeros((inputs, antennas, HALO), jnp.bfloat16)

    tiles = frames // TILE
    base = chan * (2 * antennas)
    turns = {}

    def send_rows(s, c, g, start, count):
        turns[s, c, g] = remote(
            outgoing.at[s - 1, c, pl.ds(start, count), :],
            spectra.at[c, pl.ds(pl.multiple_of(base + start, piece_rows), count), :],
            turn_send.at[s - 1, c, g], turn_recv.at[s - 1, c, g],
            (chan + s) % chan_count, tm,
        )
        turns[s, c, g].start()

    for g in range(pieces):
        loads[g].wait()

        def tile(step, _):
            @pl.when((step == tiles - 1) & (tm > 0))
            def _():
                tails[g].wait_recv()

            first = pl.multiple_of(((step + 1) % tiles) * TILE, TILE)
            block = extended[:, g * PIECE : (g + 1) * PIECE, pl.ds(first, TILE + HALO)]
            block = block.reshape(inputs * PIECE, TILE + HALO)
            shifted = [
                (pltpu.roll(block, taps - 1 - j, 1) if j < taps - 1 else block)[:, HALO:]
                for j in range(taps)
            ]
            result = jnp.dot(
                table[...], jnp.concatenate(shifted, 0), preferred_element_type=jnp.float32
            ).astype(jnp.bfloat16)
            for s in range(chan_count):
                for c in range(channels):
                    at = (s * channels + c) * piece_rows
                    part = result[at : at + piece_rows]
                    if s == 0:
                        start = pl.multiple_of(base + g * piece_rows, piece_rows)
                        spectra[c, pl.ds(start, piece_rows), pl.ds(first, TILE)] = part
                    else:
                        outgoing[s - 1, c, g * piece_rows : (g + 1) * piece_rows, pl.ds(first, TILE)] = part
            return 0

        lax.fori_loop(0, tiles, tile, 0)
        for s in range(1, chan_count):
            send_rows(s, 0, g, g * piece_rows, piece_rows)
    for c in range(1, channels):
        for s in range(1, chan_count):
            send_rows(s, c, 0, 0, pieces * piece_rows)

    spreads, chains, backs = {}, {}, {}
    half = 2 * antennas * chan_count // 2

    def part_of(index):
        return pl.ds(pl.multiple_of(index * quarter, 8), quarter)

    def own_block(c):
        for key, copy in turns.items():
            if key[1] == c:
                copy.wait_recv()
        x = spectra[c]
        product = lax.dot_general(
            x, x, (((1,), (1,)), ((), ())), preferred_element_type=jnp.float32
        )
        gram[c, :half] = product[:half, :half]
        gram[c, half : 2 * half] = product[half:, :half]
        gram[c, 2 * half :] = product[half:, half:]
        for m in range(1, PLANE):
            spreads[c, m] = remote(
                gram.at[c, part_of((spot + m) % PLANE), :], plane_in.at[c, spot],
                spread_send.at[c, m - 1], spread_recv.at[c, m - 1], chan, mate(m),
            )
            spreads[c, m].start()
        plane_in[c, spot] = gram[c, part_of(spot), :]

    def carry(c):
        for m in range(1, PLANE):
            spreads[c, m].wait_recv()
        keep = retain[c]
        total = plane_in[c, 0]
        for i in range(1, PLANE):
            total = total * keep + plane_in[c, i]
        reach = keep * keep
        reach = reach * reach
        for r in range(rounds):
            chain_out[c, r] = total
            span = PLANE**r
            for d in range(1, PLANE):
                copy = remote(
                    chain_out.at[c, r], chain_in.at[c, r, d - 1],
                    chain_send.at[c, r, d - 1], chain_recv.at[c, r, d - 1],
                    chan, tm + PLANE * span * d,
                )
                chains[c, r, d] = copy

                @pl.when(plane + span * d < plane_count)
                def _():
                    copy.start()

                @pl.when(plane < span * d)
                def _():
                    chain_in[c, r, d - 1] = jnp.zeros_like(total)

            earlier = jnp.zeros_like(total)
            for d in range(PLANE - 1, 0, -1):
                @pl.when(plane >= span * d)
                def _():
                    chains[c, r, d].wait_recv()

                earlier = earlier * reach + chain_in[c, r, d - 1]
            running = earlier if r == 0 else running + offset * earlier
            total = total + reach * earlier
            offset = reach**3 if r == 0 else offset * reach**3
            reach = reach**4
        for i in range(PLANE):
            running = running * keep + plane_in[c, i]
            plane_out[c, i] = running * inverse_weight[c, i]
        for m in range(1, PLANE):
            backs[c, m] = remote(
                plane_out.at[c, (spot + m) % PLANE], moment.at[c, part_of(spot), :],
                back_send.at[c, m - 1], back_recv.at[c, m - 1], chan, mate(m),
            )
            backs[c, m].start()
        moment[c, part_of(spot), :] = plane_out[c, spot]

    for c in range(channels):
        own_block(c)
        if c > 0:
            carry(c - 1)
    carry(channels - 1)

    for copy in backs.values():
        copy.wait()
    for copy in spreads.values():
        copy.wait_send()
    for copy in turns.values():
        copy.wait_send()

    for (c, r, d), copy in chains.items():
        @pl.when(plane + PLANE**r * d < plane_count)
        def _():
            copy.wait_send()

    @pl.when(tm + 1 < tm_count)
    def _():
        for tail in tails:
            tail.wait_send()


def turned_and_carried(volts, coef, retain, inverse_weight, taps):
    inputs, antennas, frames = volts.shape
    channels = retain.shape[0]
    chan_count, tm_count = lax.axis_size("chan"), lax.axis_size("tm")
    columns = 2 * antennas * chan_count
    half = columns // 2
    quarter = 3 * half // PLANE
    rows = coef.shape[0] * PIECE
    pieces = antennas // PIECE
    dma = pltpu.SemaphoreType.DMA
    turn_shape = (chan_count - 1, channels, pieces)
    plane_shape = (channels, PLANE - 1)
    rounds = 1
    while PLANE ** (rounds + 1) < tm_count:
        rounds += 1
    chain_shape = (channels, rounds, PLANE - 1)
    return pl.pallas_call(
        functools.partial(turn_kernel, taps, chan_count, tm_count),
        out_shape=(
            jax.ShapeDtypeStruct((channels, columns, frames), jnp.bfloat16),
            jax.ShapeDtypeStruct((channels, 3 * half, half), jnp.float32),
        ),
        in_specs=[
            pl.BlockSpec(memory_space=pltpu.HBM),
            pl.BlockSpec(memory_space=pltpu.VMEM),
            pl.BlockSpec(memory_space=pltpu.SMEM),
            pl.BlockSpec(memory_space=pltpu.SMEM),
        ],
        out_specs=(pl.BlockSpec(memory_space=pltpu.VMEM), pl.BlockSpec(memory_space=pltpu.VMEM)),
        scratch_shapes=[
            pltpu.VMEM((inputs, antennas, HALO + frames), jnp.bfloat16),
            pltpu.VMEM((rows, taps * inputs * PIECE), jnp.bfloat16),
            pltpu.VMEM((chan_count - 1, channels, 2 * antennas, frames), jnp.bfloat16),
            pltpu.VMEM((channels, 3 * half, half), jnp.float32),
            pltpu.VMEM((channels, PLANE, quarter, half), jnp.float32),
            pltpu.VMEM((channels, rounds, PLANE - 1, quarter, half), jnp.float32),
            pltpu.VMEM((channels, rounds, quarter, half), jnp.float32),
            pltpu.VMEM((channels, PLANE, quarter, half), jnp.float32),
            dma((pieces,)), dma((pieces,)), dma((pieces,)), dma(turn_shape), dma(turn_shape),
            dma(plane_shape), dma(plane_shape), dma(chain_shape), dma(chain_shape),
            dma(plane_shape), dma(plane_shape),
        ],
        compiler_params=pltpu.CompilerParams(
            collective_id=0, has_side_effects=True, vmem_limit_bytes=40 << 20
        ),
        name="turn",
    )(volts, coef, retain, inverse_weight)


def coefficient_rows(prototype, tap_count, branches, first):
    steps = np.arange(branches, dtype=np.float32)
    phase = np.float32(2.0 * math.pi / branches) * (steps[:, None] * steps[None, :])
    cosine, sine = np.cos(phase), np.sin(phase)
    pattern = np.stack([np.stack([cosine, sine], -1), np.stack([-sine, cosine], -1)], axis=1)
    pattern = np.tile(pattern.reshape(2 * branches, 2 * branches), (2, tap_count))
    pattern = lax.dynamic_slice_in_dim(jnp.asarray(pattern), 2 * first, 2 * branches, 0)
    return (jnp.repeat(prototype, 2)[None, :] * pattern).astype(jnp.bfloat16)


def per_device(voltages, prototype, forget):
    branches, parts, antennas, frames = voltages.shape
    taps = prototype.shape[0] // branches
    channels = forget.shape[0]
    tm_count = lax.axis_size("tm")
    coef = coefficient_rows(prototype, taps, branches, lax.axis_index("chan") * channels)
    rate = -forget / tm_count
    ages = jnp.arange(tm_count)
    spots = lax.axis_index("tm") // PLANE * PLANE + jnp.arange(PLANE)
    held = jnp.where(ages <= spots[:, None], 1.0, 0.0)
    powers = jnp.exp(rate[:, None] * ages.astype(jnp.float32))
    weight = frames * jnp.sum(powers[:, None, :] * held[None], -1)
    volts = voltages.reshape(branches * parts, antennas, frames)
    spectra, moment = turned_and_carried(volts, coef, jnp.exp(rate), 1.0 / weight, taps)
    return whitened_by(moment.reshape(channels, 3, BASE, BASE), spectra)


def solution(mesh):
    placed = (P(None, None, "chan", "tm"), P(), P("chan"))
    return jax.shard_map(
        per_device, mesh=mesh, in_specs=placed, out_specs=P("chan", None, "tm"), check_vma=False
    )
```

```python
import functools
import math

import jax
import jax.numpy as jnp
import numpy as np
from jax import lax
from jax.experimental import pallas as pl
from jax.experimental.pallas import tpu as pltpu
from jax.sharding import PartitionSpec as P

GROUP = 16
SUB = 8
BASE = 128


def split3(x):
    high = x.astype(jnp.bfloat16)
    rest = x - high.astype(jnp.float32)
    mid = rest.astype(jnp.bfloat16)
    low = (rest - mid.astype(jnp.float32)).astype(jnp.bfloat16)
    return high, mid, low


def exact_dot(a, b, dims):
    return lax.dot_general(
        a, b, (dims, ((), ())), precision=lax.Precision.HIGHEST, preferred_element_type=jnp.float32
    )


def eliminate(work, done, channels, beside=None):
    lane = lax.broadcasted_iota(jnp.int32, (GROUP, BASE), 1)
    row = lax.broadcasted_iota(jnp.int32, (GROUP, BASE), 0)
    below = lax.broadcasted_iota(jnp.int32, (SUB, BASE), 0)
    subs = GROUP // SUB

    def group_step(group, _):
        if beside is not None:
            beside(group)
        first = pl.multiple_of(group * GROUP, GROUP)
        trailing = (lane < BASE - first) & (lane >= GROUP)
        panels, columns, scales = [], [], []
        for c in channels:
            panel = work[c, pl.ds(first, GROUP), :]
            columns.append([
                [
                    jnp.broadcast_to(panel[h * SUB : (h + 1) * SUB, q : q + 1], (SUB, BASE))
                    for h in range(subs)
                ]
                for q in range(GROUP)
            ])
            panel = jnp.where(lane < GROUP, (lane == row).astype(jnp.float32), panel)
            panels.append([panel[h * SUB : (h + 1) * SUB] for h in range(subs)])
            scales.append([jnp.zeros((SUB, BASE), jnp.float32) for h in range(subs)])
        for p in range(GROUP):
            at, inner = p // SUB, p % SUB
            for i in range(len(channels)):
                column = columns[i]
                pivot = jnp.broadcast_to(column[p][at][inner : inner + 1, :], (SUB, BASE))
                inverse = 1.0 / pivot
                scales[i][at] = jnp.where(below == inner, inverse, scales[i][at])
                for h in range(at, subs):
                    factor = column[p][h]
                    if h == at:
                        factor = jnp.where(below > inner, factor, 0.0)
                    factor = factor * inverse
                    for part in column[p + 1 :] + [panels[i]]:
                        if h == at:
                            continue
                        part[h] = part[h] - factor * part[at][inner : inner + 1, :]
                    if h == at:
                        own = factor
                for part in column[p + 1 :] + [panels[i]]:
                    part[at] = part[at] - own * part[at][inner : inner + 1, :]
        for i, c in enumerate(channels):
            panel = jnp.concatenate(panels[i], 0)
            scale = jnp.concatenate(scales[i], 0)
            left = pltpu.roll(jnp.where(trailing, panel, 0.0), first, 1)
            lh, lm, ll = split3(left)
            rh, rm, rl = split3(panel * scale)
            lefts = jnp.concatenate([lh, lh, lh, lm, lm, ll], 0)
            rights = jnp.concatenate([rh, rm, rl, rh, rm, rh], 0)
            update = lax.dot_general(
                lefts, rights, (((0,), (0,)), ((), ())), preferred_element_type=jnp.float32
            )
            wide = lax.broadcasted_iota(jnp.int32, (BASE, BASE), 1)
            kept = jnp.where(wide < GROUP, 0.0, work[c])
            work[c] = pltpu.roll(kept - update, BASE - GROUP, 1)
            final = jnp.where(trailing, 0.0, panel) * jnp.sqrt(scale)
            done[c, pl.ds(first, GROUP), :] = pltpu.roll(final, first, 1)
        return 0

    lax.fori_loop(0, BASE // GROUP, group_step, 0)


def invert(moment, first, count, work, done, low21, high, low, beside=(None, None)):
    def block(i, at):
        return moment[first + i, at * BASE : (at + 1) * BASE]

    def store(i, down, across, value):
        rows, columns = slice(down, down + BASE), slice(across, across + BASE)
        leading = value.astype(jnp.bfloat16)
        high[i, rows, columns] = leading
        low[i, rows, columns] = (value - leading.astype(jnp.float32)).astype(jnp.bfloat16)

    for i in range(count):
        work[i] = block(i, 0)
    eliminate(work, done, range(count), beside[0])
    for i in range(count):
        inverse = done[i]
        factor = exact_dot(block(i, 1), inverse, ((1,), (1,)))
        work[i] = block(i, 2) - exact_dot(factor, factor, ((1,), (1,)))
        low21[i] = exact_dot(factor, inverse, ((1,), (0,)))
        store(i, 0, 0, inverse)
        store(i, 0, BASE, jnp.zeros_like(inverse))
    eliminate(work, done, range(count), beside[1])
    for i in range(count):
        inverse = done[i]
        store(i, BASE, 0, -exact_dot(inverse, low21[i], ((1,), (0,))))
        store(i, BASE, BASE, inverse)


def invert_scratch(count):
    square = pltpu.VMEM((max(count, 1), BASE, BASE), jnp.float32)
    return [square, square, square]


def whiten_kernel(early, moment, x_ref, early_high, early_low, out_ref, work, done, low21, high, low, result, sems):
    channels, rows, frames = x_ref.shape
    tiles = BASE // GROUP
    width = frames // tiles

    def apply(c, upper, lower, columns):
        x = x_ref[c, :, columns]
        total = jnp.dot(upper, x, preferred_element_type=jnp.float32)
        total += jnp.dot(lower, x, preferred_element_type=jnp.float32)
        result[c, :, columns] = total.astype(jnp.bfloat16)

    def tile_of(c):
        def tile(t):
            columns = pl.ds(pl.multiple_of(t * width, width), width)
            apply(c, early_high[c], early_low[c], columns)

        return tile

    copies = [pltpu.make_async_copy(result.at[c], out_ref.at[c], sems.at[c]) for c in range(channels)]
    beside = [tile_of(c) if c < early else None for c in range(2)]
    invert(moment, early, channels - early, work, done, low21, high, low, beside)
    for c in range(early):
        copies[c].start()
    for c in range(early, channels):
        apply(c, high[c - early], low[c - early], slice(None))
        copies[c].start()
    for copy in copies:
        copy.wait()


def whitened_by(moment, spectra, early_high, early_low, early):
    channels, rows, frames = spectra.shape
    late = channels - early
    parts = pltpu.VMEM((late, rows, rows), jnp.bfloat16)
    return pl.pallas_call(
        functools.partial(whiten_kernel, early),
        out_shape=jax.ShapeDtypeStruct(spectra.shape, jnp.bfloat16),
        in_specs=[pl.BlockSpec(memory_space=pltpu.VMEM)] * 4,
        out_specs=pl.BlockSpec(memory_space=pl.ANY),
        scratch_shapes=invert_scratch(late)
        + [parts, parts, pltpu.VMEM(spectra.shape, jnp.bfloat16), pltpu.SemaphoreType.DMA((channels,))],
        compiler_params=pltpu.CompilerParams(vmem_limit_bytes=40 << 20),
        name="whiten",
    )(moment, spectra, early_high, early_low)


PLANE = 4
PIECE = 16
HALO = 128
TILE = 512


def digits(shape, axis, unit, count):
    return (lax.broadcasted_iota(jnp.int32, shape, axis) // unit) % count


def turn_kernel(
    taps, chan_count, tm_count, early,
    volts, coef, retain, inverse_weight,
    spectra, moment, early_high, early_low,
    work, done, low21, extended, table, outgoing, gram, plane_in, chain_in, chain_out, plane_out,
    load_sem, halo_send, halo_recv, turn_send, turn_recv,
    spread_send, spread_recv, chain_send, chain_recv, back_send, back_recv,
):
    inputs, antennas, frames = volts.shape
    channels = spectra.shape[0]
    pieces = antennas // PIECE
    piece_rows = 2 * PIECE
    quarter = moment.shape[1] // PLANE
    chan, tm = lax.axis_index("chan"), lax.axis_index("tm")
    plane, spot = tm // PLANE, tm % PLANE
    plane_count = tm_count // PLANE
    rounds = chain_out.shape[1]

    def remote(src, dst, send, recv, chan_to, tm_to):
        return pltpu.make_async_remote_copy(
            src_ref=src, dst_ref=dst, send_sem=send, recv_sem=recv,
            device_id=(chan_to, tm_to), device_id_type=pl.DeviceIdType.MESH,
        )

    def mate(step):
        return plane * PLANE + (spot + step) % PLANE

    loads = []
    for g in range(pieces):
        rows = pl.ds(g * PIECE, PIECE)
        loads.append(
            pltpu.make_async_copy(
                volts.at[:, rows, :], extended.at[:, rows, pl.ds(HALO, frames)], load_sem.at[g]
            )
        )
        loads[-1].start()

    barrier = pltpu.get_barrier_semaphore()

    def greet(chan_to, tm_to):
        pl.semaphore_signal(
            barrier, inc=1, device_id=(chan_to, tm_to), device_id_type=pl.DeviceIdType.MESH
        )

    for s in range(1, chan_count):
        greet((chan + s) % chan_count, tm)
    for m in range(1, PLANE):
        greet(chan, mate(m))
    peers = chan_count - 1 + PLANE - 1
    hops = [PLANE**r * d for r in range(rounds) for d in range(1, PLANE)]
    meetings = [(PLANE * hop, plane + hop < plane_count) for hop in hops]
    meetings += [(-PLANE * hop, plane >= hop) for hop in hops]
    meetings.append((1, (plane + 1 < plane_count) & (spot == PLANE - 1)))
    meetings.append((-1, (plane > 0) & (spot == 0)))
    for step, reached in meetings:
        peers = peers + jnp.where(reached, 1, 0)

        @pl.when(reached)
        def _():
            greet(chan, tm + step)

    rows, columns = table.shape
    kinds, terms = coef.shape
    pick_row = digits((rows, kinds), 0, piece_rows, rows // piece_rows) * 2 + digits((rows, kinds), 0, 1, 2)
    pick_row = pick_row == lax.broadcasted_iota(jnp.int32, (rows, kinds), 1)
    pick_column = digits((terms, columns), 1, PIECE, terms)
    pick_column = pick_column == lax.broadcasted_iota(jnp.int32, (terms, columns), 0)
    spread = jnp.dot(
        pick_row.astype(jnp.float32).astype(jnp.bfloat16), coef[...], preferred_element_type=jnp.float32
    ).astype(jnp.bfloat16)
    spread = jnp.dot(
        spread, pick_column.astype(jnp.float32).astype(jnp.bfloat16), preferred_element_type=jnp.float32
    )
    own = digits((rows, columns), 0, 2, PIECE) == digits((rows, columns), 1, 1, PIECE)
    table[...] = jnp.where(own, spread, 0.0).astype(jnp.bfloat16)

    pl.semaphore_wait(barrier, peers)

    tails = []
    for g in range(pieces):
        rows = pl.ds(g * PIECE, PIECE)
        tails.append(
            remote(
                volts.at[:, rows, pl.ds(frames - HALO, HALO)], extended.at[:, rows, pl.ds(0, HALO)],
                halo_send.at[g], halo_recv.at[g], chan, tm + 1,
            )
        )

    @pl.when(tm + 1 < tm_count)
    def _():
        for tail in tails:
            tail.start()

    @pl.when(tm == 0)
    def _():
        extended[:, :, :HALO] = jnp.zeros((inputs, antennas, HALO), jnp.bfloat16)

    tiles = frames // TILE
    base = chan * (2 * antennas)
    turns = {}

    def send_rows(s, c, g, start, count):
        turns[s, c, g] = remote(
            outgoing.at[s - 1, c, pl.ds(start, count), :],
            spectra.at[c, pl.ds(pl.multiple_of(base + start, piece_rows), count), :],
            turn_send.at[s - 1, c, g], turn_recv.at[s - 1, c, g],
            (chan + s) % chan_count, tm,
        )
        turns[s, c, g].start()

    for g in range(pieces):
        loads[g].wait()

        def tile(first):
            block = extended[:, g * PIECE : (g + 1) * PIECE, pl.ds(first, TILE + HALO)]
            block = block.reshape(inputs * PIECE, TILE + HALO)
            shifted = [
                (pltpu.roll(block, taps - 1 - j, 1) if j < taps - 1 else block)[:, HALO:]
                for j in range(taps)
            ]
            return jnp.dot(
                table[...], jnp.concatenate(shifted, 0), preferred_element_type=jnp.float32
            ).astype(jnp.bfloat16)

        def store(first, result):
            for s in range(chan_count):
                for c in range(channels):
                    at = (s * channels + c) * piece_rows
                    part = result[at : at + piece_rows]
                    if s == 0:
                        start = pl.multiple_of(base + g * piece_rows, piece_rows)
                        spectra[c, pl.ds(start, piece_rows), pl.ds(first, TILE)] = part
                    else:
                        outgoing[s - 1, c, g * piece_rows : (g + 1) * piece_rows, pl.ds(first, TILE)] = part

        def pair(step, _):
            @pl.when((step == tiles // 2 - 1) & (tm > 0))
            def _():
                tails[g].wait_recv()

            places = [
                pl.multiple_of(((step * 2 + u + 1) % tiles) * TILE, TILE) for u in range(2)
            ]
            results = [tile(first) for first in places]
            for first, result in zip(places, results):
                store(first, result)
            return 0

        lax.fori_loop(0, tiles // 2, pair, 0)
        for c in range(max(early, 1)):
            for s in range(1, chan_count):
                send_rows(s, c, g, g * piece_rows, piece_rows)
    for c in range(max(early, 1), channels):
        for s in range(1, chan_count):
            send_rows(s, c, 0, 0, pieces * piece_rows)

    spreads, chains, backs = {}, {}, {}
    half = 2 * antennas * chan_count // 2

    def part_of(index):
        return pl.ds(pl.multiple_of(index * quarter, 8), quarter)

    def own_block(c):
        for key, copy in turns.items():
            if key[1] == c:
                copy.wait_recv()
        x = spectra[c]
        product = lax.dot_general(
            x, x, (((1,), (1,)), ((), ())), preferred_element_type=jnp.float32
        )
        gram[c, :half] = product[:half, :half]
        gram[c, half : 2 * half] = product[half:, :half]
        gram[c, 2 * half :] = product[half:, half:]
        for m in range(1, PLANE):
            spreads[c, m] = remote(
                gram.at[c, part_of((spot + m) % PLANE), :], plane_in.at[c, spot],
                spread_send.at[c, m - 1], spread_recv.at[c, m - 1], chan, mate(m),
            )
            spreads[c, m].start()
        plane_in[c, spot] = gram[c, part_of(spot), :]

    def carry(c):
        for m in range(1, PLANE):
            spreads[c, m].wait_recv()
        keep = retain[c]
        total = plane_in[c, 0]
        for i in range(1, PLANE):
            total = total * keep + plane_in[c, i]
        reach = keep * keep
        reach = reach * reach
        for r in range(rounds):
            chain_out[c, r] = total
            span = PLANE**r
            for d in range(1, PLANE):
                copy = remote(
                    chain_out.at[c, r], chain_in.at[c, r, d - 1],
                    chain_send.at[c, r, d - 1], chain_recv.at[c, r, d - 1],
                    chan, tm + PLANE * span * d,
                )
                chains[c, r, d] = copy

                @pl.when(plane + span * d < plane_count)
                def _():
                    copy.start()

                @pl.when(plane < span * d)
                def _():
                    chain_in[c, r, d - 1] = jnp.zeros_like(total)

            earlier = jnp.zeros_like(total)
            for d in range(PLANE - 1, 0, -1):
                @pl.when(plane >= span * d)
                def _():
                    chains[c, r, d].wait_recv()

                earlier = earlier * reach + chain_in[c, r, d - 1]
            running = earlier if r == 0 else running + offset * earlier
            total = total + reach * earlier
            offset = reach**3 if r == 0 else offset * reach**3
            reach = reach**4
        for i in range(PLANE):
            running = running * keep + plane_in[c, i]
            plane_out[c, i] = running * inverse_weight[c, i]
        for m in range(1, PLANE):
            backs[c, m] = remote(
                plane_out.at[c, (spot + m) % PLANE], moment.at[c, part_of(spot), :],
                back_send.at[c, m - 1], back_recv.at[c, m - 1], chan, mate(m),
            )
            backs[c, m].start()
        moment[c, part_of(spot), :] = plane_out[c, spot]

    for group in (range(early), range(early, channels)):
        for c in group:
            own_block(c)
        for c in group:
            carry(c)
        if group and group[0] == 0 and early:
            for (c, m), copy in backs.items():
                copy.wait()
            invert(moment, 0, early, work, done, low21, early_high, early_low)

    for (c, m), copy in backs.items():
        if c >= early:
            copy.wait()
    for copy in spreads.values():
        copy.wait_send()
    for copy in turns.values():
        copy.wait_send()

    for (c, r, d), copy in chains.items():
        @pl.when(plane + PLANE**r * d < plane_count)
        def _():
            copy.wait_send()

    @pl.when(tm + 1 < tm_count)
    def _():
        for tail in tails:
            tail.wait_send()


def turned_and_carried(volts, coef, retain, inverse_weight, taps, early):
    inputs, antennas, frames = volts.shape
    channels = retain.shape[0]
    chan_count, tm_count = lax.axis_size("chan"), lax.axis_size("tm")
    columns = 2 * antennas * chan_count
    half = columns // 2
    quarter = 3 * half // PLANE
    rows = coef.shape[0] * PIECE
    pieces = antennas // PIECE
    dma = pltpu.SemaphoreType.DMA
    turn_shape = (chan_count - 1, channels, pieces)
    plane_shape = (channels, PLANE - 1)
    rounds = 1
    while PLANE ** (rounds + 1) < tm_count:
        rounds += 1
    chain_shape = (channels, rounds, PLANE - 1)
    return pl.pallas_call(
        functools.partial(turn_kernel, taps, chan_count, tm_count, early),
        out_shape=(
            jax.ShapeDtypeStruct((channels, columns, frames), jnp.bfloat16),
            jax.ShapeDtypeStruct((channels, 3 * half, half), jnp.float32),
            jax.ShapeDtypeStruct((max(early, 1), columns, columns), jnp.bfloat16),
            jax.ShapeDtypeStruct((max(early, 1), columns, columns), jnp.bfloat16),
        ),
        in_specs=[
            pl.BlockSpec(memory_space=pltpu.HBM),
            pl.BlockSpec(memory_space=pltpu.VMEM),
            pl.BlockSpec(memory_space=pltpu.SMEM),
            pl.BlockSpec(memory_space=pltpu.SMEM),
        ],
        out_specs=(pl.BlockSpec(memory_space=pltpu.VMEM),) * 4,
        scratch_shapes=invert_scratch(early) + [
            pltpu.VMEM((inputs, antennas, HALO + frames), jnp.bfloat16),
            pltpu.VMEM((rows, taps * inputs * PIECE), jnp.bfloat16),
            pltpu.VMEM((chan_count - 1, channels, 2 * antennas, frames), jnp.bfloat16),
            pltpu.VMEM((channels, 3 * half, half), jnp.float32),
            pltpu.VMEM((channels, PLANE, quarter, half), jnp.float32),
            pltpu.VMEM((channels, rounds, PLANE - 1, quarter, half), jnp.float32),
            pltpu.VMEM((channels, rounds, quarter, half), jnp.float32),
            pltpu.VMEM((channels, PLANE, quarter, half), jnp.float32),
            dma((pieces,)), dma((pieces,)), dma((pieces,)), dma(turn_shape), dma(turn_shape),
            dma(plane_shape), dma(plane_shape), dma(chain_shape), dma(chain_shape),
            dma(plane_shape), dma(plane_shape),
        ],
        compiler_params=pltpu.CompilerParams(
            collective_id=0, has_side_effects=True, vmem_limit_bytes=40 << 20
        ),
        name="turn",
    )(volts, coef, retain, inverse_weight)


def coefficient_rows(prototype, tap_count, branches, first):
    steps = np.arange(branches, dtype=np.float32)
    phase = np.float32(2.0 * math.pi / branches) * (steps[:, None] * steps[None, :])
    cosine, sine = np.cos(phase), np.sin(phase)
    pattern = np.stack([np.stack([cosine, sine], -1), np.stack([-sine, cosine], -1)], axis=1)
    pattern = np.tile(pattern.reshape(2 * branches, 2 * branches), (2, tap_count))
    pattern = lax.dynamic_slice_in_dim(jnp.asarray(pattern), 2 * first, 2 * branches, 0)
    return (jnp.repeat(prototype, 2)[None, :] * pattern).astype(jnp.bfloat16)


def per_device(voltages, prototype, forget):
    branches, parts, antennas, frames = voltages.shape
    taps = prototype.shape[0] // branches
    channels = forget.shape[0]
    tm_count = lax.axis_size("tm")
    coef = coefficient_rows(prototype, taps, branches, lax.axis_index("chan") * channels)
    rate = -forget / tm_count
    ages = jnp.arange(tm_count)
    spots = lax.axis_index("tm") // PLANE * PLANE + jnp.arange(PLANE)
    held = jnp.where(ages <= spots[:, None], 1.0, 0.0)
    powers = jnp.exp(rate[:, None] * ages.astype(jnp.float32))
    weight = frames * jnp.sum(powers[:, None, :] * held[None], -1)
    volts = voltages.reshape(branches * parts, antennas, frames)
    early = channels // 2
    spectra, moment, high, low = turned_and_carried(
        volts, coef, jnp.exp(rate), 1.0 / weight, taps, early
    )
    return whitened_by(moment, spectra, high, low, early)


def solution(mesh):
    placed = (P(None, None, "chan", "tm"), P(), P("chan"))
    return jax.shard_map(
        per_device, mesh=mesh, in_specs=placed, out_specs=P("chan", None, "tm"), check_vma=False
    )
```

```python
import functools
import math

import jax
import jax.numpy as jnp
import numpy as np
from jax import lax
from jax.experimental import pallas as pl
from jax.experimental.pallas import tpu as pltpu
from jax.sharding import PartitionSpec as P

GROUP = 16
SUB = 8
BASE = 128


def split3(x):
    high = x.astype(jnp.bfloat16)
    rest = x - high.astype(jnp.float32)
    mid = rest.astype(jnp.bfloat16)
    low = (rest - mid.astype(jnp.float32)).astype(jnp.bfloat16)
    return high, mid, low


def exact_dot(a, b, dims):
    return lax.dot_general(
        a, b, (dims, ((), ())), precision=lax.Precision.HIGHEST, preferred_element_type=jnp.float32
    )


def eliminate(work, done, channels, beside=None):
    lane = lax.broadcasted_iota(jnp.int32, (GROUP, BASE), 1)
    row = lax.broadcasted_iota(jnp.int32, (GROUP, BASE), 0)
    below = lax.broadcasted_iota(jnp.int32, (SUB, BASE), 0)
    subs = GROUP // SUB

    def group_step(group, _):
        if beside is not None:
            beside(group)
        first = pl.multiple_of(group * GROUP, GROUP)
        trailing = (lane < BASE - first) & (lane >= GROUP)
        panels, columns, scales = [], [], []
        for c in channels:
            panel = work[c, pl.ds(first, GROUP), :]
            columns.append([
                [
                    jnp.broadcast_to(panel[h * SUB : (h + 1) * SUB, q : q + 1], (SUB, BASE))
                    for h in range(subs)
                ]
                for q in range(GROUP)
            ])
            panel = jnp.where(lane < GROUP, (lane == row).astype(jnp.float32), panel)
            panels.append([panel[h * SUB : (h + 1) * SUB] for h in range(subs)])
            scales.append([jnp.zeros((SUB, BASE), jnp.float32) for h in range(subs)])
        for p in range(GROUP):
            at, inner = p // SUB, p % SUB
            for i in range(len(channels)):
                column = columns[i]
                pivot = jnp.broadcast_to(column[p][at][inner : inner + 1, :], (SUB, BASE))
                inverse = 1.0 / pivot
                scales[i][at] = jnp.where(below == inner, inverse, scales[i][at])
                for h in range(at, subs):
                    factor = column[p][h]
                    if h == at:
                        factor = jnp.where(below > inner, factor, 0.0)
                    factor = factor * inverse
                    for part in column[p + 1 :] + [panels[i]]:
                        if h == at:
                            continue
                        part[h] = part[h] - factor * part[at][inner : inner + 1, :]
                    if h == at:
                        own = factor
                for part in column[p + 1 :] + [panels[i]]:
                    part[at] = part[at] - own * part[at][inner : inner + 1, :]
        for i, c in enumerate(channels):
            panel = jnp.concatenate(panels[i], 0)
            scale = jnp.concatenate(scales[i], 0)
            left = pltpu.roll(jnp.where(trailing, panel, 0.0), first, 1)
            lh, lm, ll = split3(left)
            rh, rm, rl = split3(panel * scale)
            lefts = jnp.concatenate([lh, lh, lh, lm, lm, ll], 0)
            rights = jnp.concatenate([rh, rm, rl, rh, rm, rh], 0)
            update = lax.dot_general(
                lefts, rights, (((0,), (0,)), ((), ())), preferred_element_type=jnp.float32
            )
            wide = lax.broadcasted_iota(jnp.int32, (BASE, BASE), 1)
            kept = jnp.where(wide < GROUP, 0.0, work[c])
            work[c] = pltpu.roll(kept - update, BASE - GROUP, 1)
            final = jnp.where(trailing, 0.0, panel) * jnp.sqrt(scale)
            done[c, pl.ds(first, GROUP), :] = pltpu.roll(final, first, 1)
        return 0

    lax.fori_loop(0, BASE // GROUP, group_step, 0)


def invert(moment, first, count, work, done, low21, high, low, beside=(None, None), between=None):
    def block(i, at):
        return moment[first + i, at * BASE : (at + 1) * BASE]

    def store(i, down, across, value):
        rows, columns = slice(down, down + BASE), slice(across, across + BASE)
        leading = value.astype(jnp.bfloat16)
        high[i, rows, columns] = leading
        low[i, rows, columns] = (value - leading.astype(jnp.float32)).astype(jnp.bfloat16)

    for i in range(count):
        work[i] = block(i, 0)
    eliminate(work, done, range(count), beside[0])
    for i in range(count):
        inverse = done[i]
        factor = exact_dot(block(i, 1), inverse, ((1,), (1,)))
        work[i] = block(i, 2) - exact_dot(factor, factor, ((1,), (1,)))
        low21[i] = exact_dot(factor, inverse, ((1,), (0,)))
        store(i, 0, 0, inverse)
        store(i, 0, BASE, jnp.zeros_like(inverse))
    if between is not None:
        between()
    eliminate(work, done, range(count), beside[1])
    for i in range(count):
        inverse = done[i]
        store(i, BASE, 0, -exact_dot(inverse, low21[i], ((1,), (0,))))
        store(i, BASE, BASE, inverse)


def invert_scratch(count):
    square = pltpu.VMEM((max(count, 1), BASE, BASE), jnp.float32)
    return [square, square, square]


def whiten_kernel(early, moment, x_ref, early_high, early_low, out_ref, work, done, low21, high, low, result, sems):
    channels, rows, frames = x_ref.shape
    tiles = BASE // GROUP
    width = frames // tiles

    def apply(c, upper, lower, columns):
        x = x_ref[c, :, columns]
        total = jnp.dot(upper, x, preferred_element_type=jnp.float32)
        total += jnp.dot(lower, x, preferred_element_type=jnp.float32)
        result[c, :, columns] = total.astype(jnp.bfloat16)

    def tile_of(c):
        def tile(t):
            columns = pl.ds(pl.multiple_of(t * width, width), width)
            apply(c, early_high[c], early_low[c], columns)

        return tile

    copies = [pltpu.make_async_copy(result.at[c], out_ref.at[c], sems.at[c]) for c in range(channels)]
    beside = [tile_of(c) if c < early else None for c in range(2)]
    invert(moment, early, channels - early, work, done, low21, high, low, beside)
    for c in range(early):
        copies[c].start()
    for c in range(early, channels):
        apply(c, high[c - early], low[c - early], slice(None))
        copies[c].start()
    for copy in copies:
        copy.wait()


def whitened_by(moment, spectra, early_high, early_low, early):
    channels, rows, frames = spectra.shape
    late = channels - early
    parts = pltpu.VMEM((late, rows, rows), jnp.bfloat16)
    return pl.pallas_call(
        functools.partial(whiten_kernel, early),
        out_shape=jax.ShapeDtypeStruct(spectra.shape, jnp.bfloat16),
        in_specs=[pl.BlockSpec(memory_space=pltpu.VMEM)] * 4,
        out_specs=pl.BlockSpec(memory_space=pl.ANY),
        scratch_shapes=invert_scratch(late)
        + [parts, parts, pltpu.VMEM(spectra.shape, jnp.bfloat16), pltpu.SemaphoreType.DMA((channels,))],
        compiler_params=pltpu.CompilerParams(vmem_limit_bytes=40 << 20),
        name="whiten",
    )(moment, spectra, early_high, early_low)


PLANE = 4
PIECE = 16
HALO = 128
TILE = 512


def digits(shape, axis, unit, count):
    return (lax.broadcasted_iota(jnp.int32, shape, axis) // unit) % count


def turn_kernel(
    taps, chan_count, tm_count, early,
    volts, coef, retain, inverse_weight,
    spectra, moment, early_high, early_low,
    work, done, low21, extended, table, outgoing, gram, plane_in, chain_in, chain_out, plane_out,
    load_sem, halo_send, halo_recv, turn_send, turn_recv,
    spread_send, spread_recv, chain_send, chain_recv, back_send, back_recv,
):
    inputs, antennas, frames = volts.shape
    channels = spectra.shape[0]
    pieces = antennas // PIECE
    piece_rows = 2 * PIECE
    quarter = moment.shape[1] // PLANE
    chan, tm = lax.axis_index("chan"), lax.axis_index("tm")
    plane, spot = tm // PLANE, tm % PLANE
    plane_count = tm_count // PLANE
    rounds = chain_out.shape[1]

    def remote(src, dst, send, recv, chan_to, tm_to):
        return pltpu.make_async_remote_copy(
            src_ref=src, dst_ref=dst, send_sem=send, recv_sem=recv,
            device_id=(chan_to, tm_to), device_id_type=pl.DeviceIdType.MESH,
        )

    def mate(step):
        return plane * PLANE + (spot + step) % PLANE

    loads = []
    for g in range(pieces):
        rows = pl.ds(g * PIECE, PIECE)
        loads.append(
            pltpu.make_async_copy(
                volts.at[:, rows, :], extended.at[:, rows, pl.ds(HALO, frames)], load_sem.at[g]
            )
        )
        loads[-1].start()

    barrier = pltpu.get_barrier_semaphore()

    def greet(chan_to, tm_to):
        pl.semaphore_signal(
            barrier, inc=1, device_id=(chan_to, tm_to), device_id_type=pl.DeviceIdType.MESH
        )

    for s in range(1, chan_count):
        greet((chan + s) % chan_count, tm)
    for m in range(1, PLANE):
        greet(chan, mate(m))
    peers = chan_count - 1 + PLANE - 1
    hops = [PLANE**r * d for r in range(rounds) for d in range(1, PLANE)]
    meetings = [(PLANE * hop, plane + hop < plane_count) for hop in hops]
    meetings += [(-PLANE * hop, plane >= hop) for hop in hops]
    meetings.append((1, (plane + 1 < plane_count) & (spot == PLANE - 1)))
    meetings.append((-1, (plane > 0) & (spot == 0)))
    for step, reached in meetings:
        peers = peers + jnp.where(reached, 1, 0)

        @pl.when(reached)
        def _():
            greet(chan, tm + step)

    rows, columns = table.shape
    kinds, terms = coef.shape
    pick_row = digits((rows, kinds), 0, piece_rows, rows // piece_rows) * 2 + digits((rows, kinds), 0, 1, 2)
    pick_row = pick_row == lax.broadcasted_iota(jnp.int32, (rows, kinds), 1)
    pick_column = digits((terms, columns), 1, PIECE, terms)
    pick_column = pick_column == lax.broadcasted_iota(jnp.int32, (terms, columns), 0)
    spread = jnp.dot(
        pick_row.astype(jnp.float32).astype(jnp.bfloat16), coef[...], preferred_element_type=jnp.float32
    ).astype(jnp.bfloat16)
    spread = jnp.dot(
        spread, pick_column.astype(jnp.float32).astype(jnp.bfloat16), preferred_element_type=jnp.float32
    )
    own = digits((rows, columns), 0, 2, PIECE) == digits((rows, columns), 1, 1, PIECE)
    table[...] = jnp.where(own, spread, 0.0).astype(jnp.bfloat16)

    pl.semaphore_wait(barrier, peers)

    tails = []
    for g in range(pieces):
        rows = pl.ds(g * PIECE, PIECE)
        tails.append(
            remote(
                volts.at[:, rows, pl.ds(frames - HALO, HALO)], extended.at[:, rows, pl.ds(0, HALO)],
                halo_send.at[g], halo_recv.at[g], chan, tm + 1,
            )
        )

    @pl.when(tm + 1 < tm_count)
    def _():
        for tail in tails:
            tail.start()

    @pl.when(tm == 0)
    def _():
        extended[:, :, :HALO] = jnp.zeros((inputs, antennas, HALO), jnp.bfloat16)

    tiles = frames // TILE
    base = chan * (2 * antennas)
    turns = {}

    def send_rows(s, c, g, start, count):
        turns[s, c, g] = remote(
            outgoing.at[s - 1, c, pl.ds(start, count), :],
            spectra.at[c, pl.ds(pl.multiple_of(base + start, piece_rows), count), :],
            turn_send.at[s - 1, c, g], turn_recv.at[s - 1, c, g],
            (chan + s) % chan_count, tm,
        )
        turns[s, c, g].start()

    for g in range(pieces):
        loads[g].wait()

        def tile(first):
            block = extended[:, g * PIECE : (g + 1) * PIECE, pl.ds(first, TILE + HALO)]
            block = block.reshape(inputs * PIECE, TILE + HALO)
            shifted = [
                (pltpu.roll(block, taps - 1 - j, 1) if j < taps - 1 else block)[:, HALO:]
                for j in range(taps)
            ]
            return jnp.dot(
                table[...], jnp.concatenate(shifted, 0), preferred_element_type=jnp.float32
            ).astype(jnp.bfloat16)

        def store(first, result):
            for s in range(chan_count):
                for c in range(channels):
                    at = (s * channels + c) * piece_rows
                    part = result[at : at + piece_rows]
                    if s == 0:
                        start = pl.multiple_of(base + g * piece_rows, piece_rows)
                        spectra[c, pl.ds(start, piece_rows), pl.ds(first, TILE)] = part
                    else:
                        outgoing[s - 1, c, g * piece_rows : (g + 1) * piece_rows, pl.ds(first, TILE)] = part

        def pair(step, _):
            @pl.when((step == tiles // 2 - 1) & (tm > 0))
            def _():
                tails[g].wait_recv()

            places = [
                pl.multiple_of(((step * 2 + u + 1) % tiles) * TILE, TILE) for u in range(2)
            ]
            results = [tile(first) for first in places]
            for first, result in zip(places, results):
                store(first, result)
            return 0

        lax.fori_loop(0, tiles // 2, pair, 0)
        for c in range(max(early, 1)):
            for s in range(1, chan_count):
                send_rows(s, c, g, g * piece_rows, piece_rows)
    for c in range(max(early, 1), channels):
        for s in range(1, chan_count):
            send_rows(s, c, 0, 0, pieces * piece_rows)

    spreads, chains, backs = {}, {}, {}
    half = 2 * antennas * chan_count // 2

    def part_of(index):
        return pl.ds(pl.multiple_of(index * quarter, 8), quarter)

    def own_block(c):
        for key, copy in turns.items():
            if key[1] == c:
                copy.wait_recv()
        x = spectra[c]
        product = lax.dot_general(
            x, x, (((1,), (1,)), ((), ())), preferred_element_type=jnp.float32
        )
        gram[c, :half] = product[:half, :half]
        gram[c, half : 2 * half] = product[half:, :half]
        gram[c, 2 * half :] = product[half:, half:]
        for m in range(1, PLANE):
            spreads[c, m] = remote(
                gram.at[c, part_of((spot + m) % PLANE), :], plane_in.at[c, spot],
                spread_send.at[c, m - 1], spread_recv.at[c, m - 1], chan, mate(m),
            )
            spreads[c, m].start()
        plane_in[c, spot] = gram[c, part_of(spot), :]

    def pass_on(c):
        for m in range(1, PLANE):
            spreads[c, m].wait_recv()
        keep = retain[c]
        total = plane_in[c, 0]
        for i in range(1, PLANE):
            total = total * keep + plane_in[c, i]
        send_total(c, 0, total)

    def send_total(c, r, total):
        chain_out[c, r] = total
        span = PLANE**r
        for d in range(1, PLANE):
            copy = remote(
                chain_out.at[c, r], chain_in.at[c, r, d - 1],
                chain_send.at[c, r, d - 1], chain_recv.at[c, r, d - 1],
                chan, tm + PLANE * span * d,
            )
            chains[c, r, d] = copy

            @pl.when(plane + span * d < plane_count)
            def _():
                copy.start()

            @pl.when(plane < span * d)
            def _():
                chain_in[c, r, d - 1] = jnp.zeros_like(total)

    def carry(c):
        keep = retain[c]
        reach = keep * keep
        reach = reach * reach
        for r in range(rounds):
            span = PLANE**r
            earlier = jnp.zeros(chain_out.shape[2:], jnp.float32)
            for d in range(PLANE - 1, 0, -1):
                @pl.when(plane >= span * d)
                def _():
                    chains[c, r, d].wait_recv()

                earlier = earlier * reach + chain_in[c, r, d - 1]
            running = earlier if r == 0 else running + offset * earlier
            if r + 1 < rounds:
                send_total(c, r + 1, chain_out[c, r] + reach * earlier)
            offset = reach**3 if r == 0 else offset * reach**3
            reach = reach**4
        for i in range(PLANE):
            running = running * keep + plane_in[c, i]
            plane_out[c, i] = running * inverse_weight[c, i]
        for m in range(1, PLANE):
            backs[c, m] = remote(
                plane_out.at[c, (spot + m) % PLANE], moment.at[c, part_of(spot), :],
                back_send.at[c, m - 1], back_recv.at[c, m - 1], chan, mate(m),
            )
            backs[c, m].start()
        moment[c, part_of(spot), :] = plane_out[c, spot]

    def early_part():
        for c in range(early):
            own_block(c)
        for c in range(early):
            pass_on(c)
        for c in range(early):
            carry(c)
        for copy in backs.values():
            copy.wait()

    if early:
        early_part()
        invert(
            moment, 0, early, work, done, low21, early_high, early_low,
            between=lambda: own_block(early),
        )
    else:
        own_block(0)
    pass_on(early)
    for c in range(early, channels):
        if c + 1 < channels:
            own_block(c + 1)
        carry(c)
        if c + 1 < channels:
            pass_on(c + 1)

    for (c, m), copy in backs.items():
        if c >= early:
            copy.wait()
    for copy in spreads.values():
        copy.wait_send()
    for copy in turns.values():
        copy.wait_send()

    for (c, r, d), copy in chains.items():
        @pl.when(plane + PLANE**r * d < plane_count)
        def _():
            copy.wait_send()

    @pl.when(tm + 1 < tm_count)
    def _():
        for tail in tails:
            tail.wait_send()


def turned_and_carried(volts, coef, retain, inverse_weight, taps, early):
    inputs, antennas, frames = volts.shape
    channels = retain.shape[0]
    chan_count, tm_count = lax.axis_size("chan"), lax.axis_size("tm")
    columns = 2 * antennas * chan_count
    half = columns // 2
    quarter = 3 * half // PLANE
    rows = coef.shape[0] * PIECE
    pieces = antennas // PIECE
    dma = pltpu.SemaphoreType.DMA
    turn_shape = (chan_count - 1, channels, pieces)
    plane_shape = (channels, PLANE - 1)
    rounds = 1
    while PLANE ** (rounds + 1) < tm_count:
        rounds += 1
    chain_shape = (channels, rounds, PLANE - 1)
    return pl.pallas_call(
        functools.partial(turn_kernel, taps, chan_count, tm_count, early),
        out_shape=(
            jax.ShapeDtypeStruct((channels, columns, frames), jnp.bfloat16),
            jax.ShapeDtypeStruct((channels, 3 * half, half), jnp.float32),
            jax.ShapeDtypeStruct((max(early, 1), columns, columns), jnp.bfloat16),
            jax.ShapeDtypeStruct((max(early, 1), columns, columns), jnp.bfloat16),
        ),
        in_specs=[
            pl.BlockSpec(memory_space=pltpu.HBM),
            pl.BlockSpec(memory_space=pltpu.VMEM),
            pl.BlockSpec(memory_space=pltpu.SMEM),
            pl.BlockSpec(memory_space=pltpu.SMEM),
        ],
        out_specs=(pl.BlockSpec(memory_space=pltpu.VMEM),) * 4,
        scratch_shapes=invert_scratch(early) + [
            pltpu.VMEM((inputs, antennas, HALO + frames), jnp.bfloat16),
            pltpu.VMEM((rows, taps * inputs * PIECE), jnp.bfloat16),
            pltpu.VMEM((chan_count - 1, channels, 2 * antennas, frames), jnp.bfloat16),
            pltpu.VMEM((channels, 3 * half, half), jnp.float32),
            pltpu.VMEM((channels, PLANE, quarter, half), jnp.float32),
            pltpu.VMEM((channels, rounds, PLANE - 1, quarter, half), jnp.float32),
            pltpu.VMEM((channels, rounds, quarter, half), jnp.float32),
            pltpu.VMEM((channels, PLANE, quarter, half), jnp.float32),
            dma((pieces,)), dma((pieces,)), dma((pieces,)), dma(turn_shape), dma(turn_shape),
            dma(plane_shape), dma(plane_shape), dma(chain_shape), dma(chain_shape),
            dma(plane_shape), dma(plane_shape),
        ],
        compiler_params=pltpu.CompilerParams(
            collective_id=0, has_side_effects=True, vmem_limit_bytes=47 << 20
        ),
        name="turn",
    )(volts, coef, retain, inverse_weight)


def coefficient_rows(prototype, tap_count, branches, first):
    steps = np.arange(branches, dtype=np.float32)
    phase = np.float32(2.0 * math.pi / branches) * (steps[:, None] * steps[None, :])
    cosine, sine = np.cos(phase), np.sin(phase)
    pattern = np.stack([np.stack([cosine, sine], -1), np.stack([-sine, cosine], -1)], axis=1)
    pattern = np.tile(pattern.reshape(2 * branches, 2 * branches), (2, tap_count))
    pattern = lax.dynamic_slice_in_dim(jnp.asarray(pattern), 2 * first, 2 * branches, 0)
    return (jnp.repeat(prototype, 2)[None, :] * pattern).astype(jnp.bfloat16)


def per_device(voltages, prototype, forget):
    branches, parts, antennas, frames = voltages.shape
    taps = prototype.shape[0] // branches
    channels = forget.shape[0]
    tm_count = lax.axis_size("tm")
    coef = coefficient_rows(prototype, taps, branches, lax.axis_index("chan") * channels)
    rate = -forget / tm_count
    ages = jnp.arange(tm_count)
    spots = lax.axis_index("tm") // PLANE * PLANE + jnp.arange(PLANE)
    held = jnp.where(ages <= spots[:, None], 1.0, 0.0)
    powers = jnp.exp(rate[:, None] * ages.astype(jnp.float32))
    weight = frames * jnp.sum(powers[:, None, :] * held[None], -1)
    volts = voltages.reshape(branches * parts, antennas, frames)
    early = channels // 2
    spectra, moment, high, low = turned_and_carried(
        volts, coef, jnp.exp(rate), 1.0 / weight, taps, early
    )
    return whitened_by(moment, spectra, high, low, early)


def solution(mesh):
    placed = (P(None, None, "chan", "tm"), P(), P("chan"))
    return jax.shard_map(
        per_device, mesh=mesh, in_specs=placed, out_specs=P("chan", None, "tm"), check_vma=False
    )
```

```python
import functools
import math

import jax
import jax.numpy as jnp
import numpy as np
from jax import lax
from jax.experimental import pallas as pl
from jax.experimental.pallas import tpu as pltpu
from jax.sharding import PartitionSpec as P

GROUP = 16
SUB = 8
BASE = 128


def split3(x):
    high = x.astype(jnp.bfloat16)
    rest = x - high.astype(jnp.float32)
    mid = rest.astype(jnp.bfloat16)
    low = (rest - mid.astype(jnp.float32)).astype(jnp.bfloat16)
    return high, mid, low


def exact_dot(a, b, dims):
    return lax.dot_general(
        a, b, (dims, ((), ())), precision=lax.Precision.HIGHEST, preferred_element_type=jnp.float32
    )


def eliminate(work, done, channels, beside=None):
    lane = lax.broadcasted_iota(jnp.int32, (GROUP, BASE), 1)
    row = lax.broadcasted_iota(jnp.int32, (GROUP, BASE), 0)
    below = lax.broadcasted_iota(jnp.int32, (SUB, BASE), 0)
    subs = GROUP // SUB

    def group_step(group, _):
        if beside is not None:
            beside(group)
        first = pl.multiple_of(group * GROUP, GROUP)
        trailing = (lane < BASE - first) & (lane >= GROUP)
        panels, columns, scales = [], [], []
        for c in channels:
            panel = work[c, pl.ds(first, GROUP), :]
            columns.append([
                [
                    jnp.broadcast_to(panel[h * SUB : (h + 1) * SUB, q : q + 1], (SUB, BASE))
                    for h in range(subs)
                ]
                for q in range(GROUP)
            ])
            panel = jnp.where(lane < GROUP, (lane == row).astype(jnp.float32), panel)
            panels.append([panel[h * SUB : (h + 1) * SUB] for h in range(subs)])
            scales.append([jnp.zeros((SUB, BASE), jnp.float32) for h in range(subs)])
        for p in range(GROUP):
            at, inner = p // SUB, p % SUB
            for i in range(len(channels)):
                column = columns[i]
                pivot = jnp.broadcast_to(column[p][at][inner : inner + 1, :], (SUB, BASE))
                inverse = pl.reciprocal(pivot)
                scales[i][at] = jnp.where(below == inner, inverse, scales[i][at])
                for h in range(at, subs):
                    factor = column[p][h]
                    if h == at:
                        factor = jnp.where(below > inner, factor, 0.0)
                    factor = factor * inverse
                    for part in column[p + 1 :] + [panels[i]]:
                        if h == at:
                            continue
                        part[h] = part[h] - factor * part[at][inner : inner + 1, :]
                    if h == at:
                        own = factor
                for part in column[p + 1 :] + [panels[i]]:
                    part[at] = part[at] - own * part[at][inner : inner + 1, :]
        for i, c in enumerate(channels):
            panel = jnp.concatenate(panels[i], 0)
            scale = jnp.concatenate(scales[i], 0)
            left = pltpu.roll(jnp.where(trailing, panel, 0.0), first, 1)
            lh, lm, ll = split3(left)
            rh, rm, rl = split3(panel * scale)
            lefts = jnp.concatenate([lh, lh, lh, lm, lm, ll], 0)
            rights = jnp.concatenate([rh, rm, rl, rh, rm, rh], 0)
            update = lax.dot_general(
                lefts, rights, (((0,), (0,)), ((), ())), preferred_element_type=jnp.float32
            )
            wide = lax.broadcasted_iota(jnp.int32, (BASE, BASE), 1)
            kept = jnp.where(wide < GROUP, 0.0, work[c])
            work[c] = pltpu.roll(kept - update, BASE - GROUP, 1)
            final = jnp.where(trailing, 0.0, panel) * jnp.sqrt(scale)
            done[c, pl.ds(first, GROUP), :] = pltpu.roll(final, first, 1)
        return 0

    lax.fori_loop(0, BASE // GROUP, group_step, 0)


def invert(moment, first, count, work, done, low21, high, low, beside=(None, None), between=None):
    def block(i, at):
        return moment[first + i, at * BASE : (at + 1) * BASE]

    def store(i, down, across, value):
        rows, columns = slice(down, down + BASE), slice(across, across + BASE)
        leading = value.astype(jnp.bfloat16)
        high[i, rows, columns] = leading
        low[i, rows, columns] = (value - leading.astype(jnp.float32)).astype(jnp.bfloat16)

    for i in range(count):
        work[i] = block(i, 0)
    eliminate(work, done, range(count), beside[0])
    for i in range(count):
        inverse = done[i]
        factor = exact_dot(block(i, 1), inverse, ((1,), (1,)))
        work[i] = block(i, 2) - exact_dot(factor, factor, ((1,), (1,)))
        low21[i] = exact_dot(factor, inverse, ((1,), (0,)))
        store(i, 0, 0, inverse)
        store(i, 0, BASE, jnp.zeros_like(inverse))
    if between is not None:
        between()
    eliminate(work, done, range(count), beside[1])
    for i in range(count):
        inverse = done[i]
        store(i, BASE, 0, -exact_dot(inverse, low21[i], ((1,), (0,))))
        store(i, BASE, BASE, inverse)


def invert_scratch(count):
    square = pltpu.VMEM((max(count, 1), BASE, BASE), jnp.float32)
    return [square, square, square]


def whiten_kernel(early, moment, x_ref, early_high, early_low, out_ref, work, done, low21, high, low, result, sems):
    channels, rows, frames = x_ref.shape
    tiles = BASE // GROUP
    width = frames // tiles

    def apply(c, upper, lower, columns):
        x = x_ref[c, :, columns]
        total = jnp.dot(upper, x, preferred_element_type=jnp.float32)
        total += jnp.dot(lower, x, preferred_element_type=jnp.float32)
        result[c, :, columns] = total.astype(jnp.bfloat16)

    def tile_of(c):
        def tile(t):
            columns = pl.ds(pl.multiple_of(t * width, width), width)
            apply(c, early_high[c], early_low[c], columns)

        return tile

    copies = [pltpu.make_async_copy(result.at[c], out_ref.at[c], sems.at[c]) for c in range(channels)]
    beside = [tile_of(c) if c < early else None for c in range(2)]
    invert(
        moment, early, channels - early, work, done, low21, high, low, beside,
        between=copies[0].start if early else None,
    )
    for c in range(1, early):
        copies[c].start()
    for c in range(early, channels):
        apply(c, high[c - early], low[c - early], slice(None))
        copies[c].start()
    for copy in copies:
        copy.wait()


def whitened_by(moment, spectra, early_high, early_low, early):
    channels, rows, frames = spectra.shape
    late = channels - early
    parts = pltpu.VMEM((late, rows, rows), jnp.bfloat16)
    return pl.pallas_call(
        functools.partial(whiten_kernel, early),
        out_shape=jax.ShapeDtypeStruct(spectra.shape, jnp.bfloat16),
        in_specs=[pl.BlockSpec(memory_space=pltpu.VMEM)] * 4,
        out_specs=pl.BlockSpec(memory_space=pl.ANY),
        scratch_shapes=invert_scratch(late)
        + [parts, parts, pltpu.VMEM(spectra.shape, jnp.bfloat16), pltpu.SemaphoreType.DMA((channels,))],
        compiler_params=pltpu.CompilerParams(vmem_limit_bytes=40 << 20),
        name="whiten",
    )(moment, spectra, early_high, early_low)


PLANE = 4
PIECE = 16
HALO = 128
TILE = 512


def digits(shape, axis, unit, count):
    return (lax.broadcasted_iota(jnp.int32, shape, axis) // unit) % count


def turn_kernel(
    taps, chan_count, tm_count, early,
    volts, coef, retain, inverse_weight,
    spectra, moment, early_high, early_low,
    work, done, low21, extended, table, outgoing, gram, plane_in, chain_in, chain_out, plane_out,
    load_sem, halo_send, halo_recv, turn_send, turn_recv,
    spread_send, spread_recv, chain_send, chain_recv, back_send, back_recv,
):
    inputs, antennas, frames = volts.shape
    channels = spectra.shape[0]
    pieces = antennas // PIECE
    piece_rows = 2 * PIECE
    quarter = moment.shape[1] // PLANE
    chan, tm = lax.axis_index("chan"), lax.axis_index("tm")
    plane, spot = tm // PLANE, tm % PLANE
    plane_count = tm_count // PLANE
    rounds = chain_out.shape[1]

    def remote(src, dst, send, recv, chan_to, tm_to):
        return pltpu.make_async_remote_copy(
            src_ref=src, dst_ref=dst, send_sem=send, recv_sem=recv,
            device_id=(chan_to, tm_to), device_id_type=pl.DeviceIdType.MESH,
        )

    def mate(step):
        return plane * PLANE + (spot + step) % PLANE

    loads = []
    for g in range(pieces):
        rows = pl.ds(g * PIECE, PIECE)
        loads.append(
            pltpu.make_async_copy(
                volts.at[:, rows, :], extended.at[:, rows, pl.ds(HALO, frames)], load_sem.at[g]
            )
        )
        loads[-1].start()

    barrier = pltpu.get_barrier_semaphore()

    def greet(chan_to, tm_to):
        pl.semaphore_signal(
            barrier, inc=1, device_id=(chan_to, tm_to), device_id_type=pl.DeviceIdType.MESH
        )

    for s in range(1, chan_count):
        greet((chan + s) % chan_count, tm)
    for m in range(1, PLANE):
        greet(chan, mate(m))
    peers = chan_count - 1 + PLANE - 1
    hops = [PLANE**r * d for r in range(rounds) for d in range(1, PLANE)]
    meetings = [(PLANE * hop, plane + hop < plane_count) for hop in hops]
    meetings += [(-PLANE * hop, plane >= hop) for hop in hops]
    meetings.append((1, (plane + 1 < plane_count) & (spot == PLANE - 1)))
    meetings.append((-1, (plane > 0) & (spot == 0)))
    for step, reached in meetings:
        peers = peers + jnp.where(reached, 1, 0)

        @pl.when(reached)
        def _():
            greet(chan, tm + step)

    rows, columns = table.shape
    kinds, terms = coef.shape
    pick_row = digits((rows, kinds), 0, piece_rows, rows // piece_rows) * 2 + digits((rows, kinds), 0, 1, 2)
    pick_row = pick_row == lax.broadcasted_iota(jnp.int32, (rows, kinds), 1)
    pick_column = digits((terms, columns), 1, PIECE, terms)
    pick_column = pick_column == lax.broadcasted_iota(jnp.int32, (terms, columns), 0)
    spread = jnp.dot(
        pick_row.astype(jnp.float32).astype(jnp.bfloat16), coef[...], preferred_element_type=jnp.float32
    ).astype(jnp.bfloat16)
    spread = jnp.dot(
        spread, pick_column.astype(jnp.float32).astype(jnp.bfloat16), preferred_element_type=jnp.float32
    )
    own = digits((rows, columns), 0, 2, PIECE) == digits((rows, columns), 1, 1, PIECE)
    table[...] = jnp.where(own, spread, 0.0).astype(jnp.bfloat16)

    pl.semaphore_wait(barrier, peers)

    tails = []
    for g in range(pieces):
        rows = pl.ds(g * PIECE, PIECE)
        tails.append(
            remote(
                volts.at[:, rows, pl.ds(frames - HALO, HALO)], extended.at[:, rows, pl.ds(0, HALO)],
                halo_send.at[g], halo_recv.at[g], chan, tm + 1,
            )
        )

    @pl.when(tm + 1 < tm_count)
    def _():
        for tail in tails:
            tail.start()

    @pl.when(tm == 0)
    def _():
        extended[:, :, :HALO] = jnp.zeros((inputs, antennas, HALO), jnp.bfloat16)

    tiles = frames // TILE
    base = chan * (2 * antennas)
    pairs = tiles // 2
    turns = []

    def turn_copy(s, c, slot, start, count, first, width):
        lanes = pl.ds(first, width)
        return remote(
            outgoing.at[s - 1, c, pl.ds(start, count), lanes],
            spectra.at[c, pl.ds(pl.multiple_of(base + start, piece_rows), count), lanes],
            turn_send.at[s - 1, c, slot], turn_recv.at[s - 1, c, slot],
            (chan + s) % chan_count, tm,
        )

    for g in range(pieces):
        loads[g].wait()

        def tile(first):
            block = extended[:, g * PIECE : (g + 1) * PIECE, pl.ds(first, TILE + HALO)]
            block = block.reshape(inputs * PIECE, TILE + HALO)
            shifted = [
                (pltpu.roll(block, taps - 1 - j, 1) if j < taps - 1 else block)[:, HALO:]
                for j in range(taps)
            ]
            return jnp.dot(
                table[...], jnp.concatenate(shifted, 0), preferred_element_type=jnp.float32
            ).astype(jnp.bfloat16)

        def store(first, result):
            for s in range(chan_count):
                for c in range(channels):
                    at = (s * channels + c) * piece_rows
                    part = result[at : at + piece_rows]
                    if s == 0:
                        start = pl.multiple_of(base + g * piece_rows, piece_rows)
                        spectra[c, pl.ds(start, piece_rows), pl.ds(first, TILE)] = part
                    else:
                        outgoing[s - 1, c, g * piece_rows : (g + 1) * piece_rows, pl.ds(first, TILE)] = part

        def pair(step, _):
            @pl.when((step == pairs - 1) & (tm > 0))
            def _():
                tails[g].wait_recv()

            start = pl.multiple_of((pairs - 1 - step) * (2 * TILE), 2 * TILE)
            places = [pl.multiple_of(start + u * TILE, TILE) for u in range(2)]
            results = [tile(first) for first in places]
            for first, result in zip(places, results):
                store(first, result)
            for c in range(max(early, 1)):
                for s in range(1, chan_count):
                    turn_copy(
                        s, c, g * pairs + step, g * piece_rows, piece_rows, start, 2 * TILE
                    ).start()
            return 0

        lax.fori_loop(0, pairs, pair, 0)
        for c in range(max(early, 1)):
            for s in range(1, chan_count):
                for step in range(pairs):
                    first = (pairs - 1 - step) * (2 * TILE)
                    slot = g * pairs + step
                    turns.append(
                        (c, turn_copy(s, c, slot, g * piece_rows, piece_rows, first, 2 * TILE))
                    )
    for c in range(max(early, 1), channels):
        for s in range(1, chan_count):
            turns.append((c, turn_copy(s, c, 0, 0, pieces * piece_rows, 0, frames)))
            turns[-1][1].start()

    spreads, chains, backs = {}, {}, {}
    half = 2 * antennas * chan_count // 2

    def part_of(index):
        return pl.ds(pl.multiple_of(index * quarter, 8), quarter)

    def own_block(c):
        for owner, copy in turns:
            if owner == c:
                copy.wait_recv()
        x = spectra[c]
        product = lax.dot_general(
            x, x, (((1,), (1,)), ((), ())), preferred_element_type=jnp.float32
        )
        gram[c, :half] = product[:half, :half]
        gram[c, half : 2 * half] = product[half:, :half]
        gram[c, 2 * half :] = product[half:, half:]
        for m in range(1, PLANE):
            spreads[c, m] = remote(
                gram.at[c, part_of((spot + m) % PLANE), :], plane_in.at[c, spot],
                spread_send.at[c, m - 1], spread_recv.at[c, m - 1], chan, mate(m),
            )
            spreads[c, m].start()
        plane_in[c, spot] = gram[c, part_of(spot), :]

    def pass_on(c):
        for m in range(1, PLANE):
            spreads[c, m].wait_recv()
        keep = retain[c]
        total = plane_in[c, 0]
        for i in range(1, PLANE):
            total = total * keep + plane_in[c, i]
        send_total(c, 0, total)

    def send_total(c, r, total):
        chain_out[c, r] = total
        span = PLANE**r
        for d in range(1, PLANE):
            copy = remote(
                chain_out.at[c, r], chain_in.at[c, r, d - 1],
                chain_send.at[c, r, d - 1], chain_recv.at[c, r, d - 1],
                chan, tm + PLANE * span * d,
            )
            chains[c, r, d] = copy

            @pl.when(plane + span * d < plane_count)
            def _():
                copy.start()

            @pl.when(plane < span * d)
            def _():
                chain_in[c, r, d - 1] = jnp.zeros_like(total)

    def carry(c):
        keep = retain[c]
        reach = keep * keep
        reach = reach * reach
        for r in range(rounds):
            span = PLANE**r
            earlier = jnp.zeros(chain_out.shape[2:], jnp.float32)
            for d in range(PLANE - 1, 0, -1):
                @pl.when(plane >= span * d)
                def _():
                    chains[c, r, d].wait_recv()

                earlier = earlier * reach + chain_in[c, r, d - 1]
            running = earlier if r == 0 else running + offset * earlier
            if r + 1 < rounds:
                send_total(c, r + 1, chain_out[c, r] + reach * earlier)
            offset = reach**3 if r == 0 else offset * reach**3
            reach = reach**4
        for i in range(PLANE):
            running = running * keep + plane_in[c, i]
            plane_out[c, i] = running * inverse_weight[c, i]
        for m in range(1, PLANE):
            backs[c, m] = remote(
                plane_out.at[c, (spot + m) % PLANE], moment.at[c, part_of(spot), :],
                back_send.at[c, m - 1], back_recv.at[c, m - 1], chan, mate(m),
            )
            backs[c, m].start()
        moment[c, part_of(spot), :] = plane_out[c, spot]

    def early_part():
        for c in range(early):
            own_block(c)
        for c in range(early):
            pass_on(c)
        for c in range(early):
            carry(c)
        for copy in backs.values():
            copy.wait()

    if early:
        early_part()
        invert(
            moment, 0, early, work, done, low21, early_high, early_low,
            between=lambda: own_block(early),
        )
    else:
        own_block(0)
    pass_on(early)
    for c in range(early, channels):
        if c + 1 < channels:
            own_block(c + 1)
        carry(c)
        if c + 1 < channels:
            pass_on(c + 1)

    for (c, m), copy in backs.items():
        if c >= early:
            copy.wait()
    for copy in spreads.values():
        copy.wait_send()
    for _, copy in turns:
        copy.wait_send()

    for (c, r, d), copy in chains.items():
        @pl.when(plane + PLANE**r * d < plane_count)
        def _():
            copy.wait_send()

    @pl.when(tm + 1 < tm_count)
    def _():
        for tail in tails:
            tail.wait_send()


def turned_and_carried(volts, coef, retain, inverse_weight, taps, early):
    inputs, antennas, frames = volts.shape
    channels = retain.shape[0]
    chan_count, tm_count = lax.axis_size("chan"), lax.axis_size("tm")
    columns = 2 * antennas * chan_count
    half = columns // 2
    quarter = 3 * half // PLANE
    rows = coef.shape[0] * PIECE
    pieces = antennas // PIECE
    dma = pltpu.SemaphoreType.DMA
    turn_shape = (chan_count - 1, channels, pieces * (frames // (2 * TILE)))
    plane_shape = (channels, PLANE - 1)
    rounds = 1
    while PLANE ** (rounds + 1) < tm_count:
        rounds += 1
    chain_shape = (channels, rounds, PLANE - 1)
    return pl.pallas_call(
        functools.partial(turn_kernel, taps, chan_count, tm_count, early),
        out_shape=(
            jax.ShapeDtypeStruct((channels, columns, frames), jnp.bfloat16),
            jax.ShapeDtypeStruct((channels, 3 * half, half), jnp.float32),
            jax.ShapeDtypeStruct((max(early, 1), columns, columns), jnp.bfloat16),
            jax.ShapeDtypeStruct((max(early, 1), columns, columns), jnp.bfloat16),
        ),
        in_specs=[
            pl.BlockSpec(memory_space=pltpu.HBM),
            pl.BlockSpec(memory_space=pltpu.VMEM),
            pl.BlockSpec(memory_space=pltpu.SMEM),
            pl.BlockSpec(memory_space=pltpu.SMEM),
        ],
        out_specs=(pl.BlockSpec(memory_space=pltpu.VMEM),) * 4,
        scratch_shapes=invert_scratch(early) + [
            pltpu.VMEM((inputs, antennas, HALO + frames), jnp.bfloat16),
            pltpu.VMEM((rows, taps * inputs * PIECE), jnp.bfloat16),
            pltpu.VMEM((chan_count - 1, channels, 2 * antennas, frames), jnp.bfloat16),
            pltpu.VMEM((channels, 3 * half, half), jnp.float32),
            pltpu.VMEM((channels, PLANE, quarter, half), jnp.float32),
            pltpu.VMEM((channels, rounds, PLANE - 1, quarter, half), jnp.float32),
            pltpu.VMEM((channels, rounds, quarter, half), jnp.float32),
            pltpu.VMEM((channels, PLANE, quarter, half), jnp.float32),
            dma((pieces,)), dma((pieces,)), dma((pieces,)), dma(turn_shape), dma(turn_shape),
            dma(plane_shape), dma(plane_shape), dma(chain_shape), dma(chain_shape),
            dma(plane_shape), dma(plane_shape),
        ],
        compiler_params=pltpu.CompilerParams(
            collective_id=0, has_side_effects=True, vmem_limit_bytes=47 << 20
        ),
        name="turn",
    )(volts, coef, retain, inverse_weight)


def coefficient_rows(prototype, tap_count, branches, first):
    steps = np.arange(branches, dtype=np.float32)
    phase = np.float32(2.0 * math.pi / branches) * (steps[:, None] * steps[None, :])
    cosine, sine = np.cos(phase), np.sin(phase)
    pattern = np.stack([np.stack([cosine, sine], -1), np.stack([-sine, cosine], -1)], axis=1)
    pattern = np.tile(pattern.reshape(2 * branches, 2 * branches), (2, tap_count))
    pattern = lax.dynamic_slice_in_dim(jnp.asarray(pattern), 2 * first, 2 * branches, 0)
    return (jnp.repeat(prototype, 2)[None, :] * pattern).astype(jnp.bfloat16)


def per_device(voltages, prototype, forget):
    branches, parts, antennas, frames = voltages.shape
    taps = prototype.shape[0] // branches
    channels = forget.shape[0]
    tm_count = lax.axis_size("tm")
    coef = coefficient_rows(prototype, taps, branches, lax.axis_index("chan") * channels)
    rate = -forget / tm_count
    ages = jnp.arange(tm_count)
    spots = lax.axis_index("tm") // PLANE * PLANE + jnp.arange(PLANE)
    held = jnp.where(ages <= spots[:, None], 1.0, 0.0)
    powers = jnp.exp(rate[:, None] * ages.astype(jnp.float32))
    weight = frames * jnp.sum(powers[:, None, :] * held[None], -1)
    volts = voltages.reshape(branches * parts, antennas, frames)
    early = channels // 2
    spectra, moment, high, low = turned_and_carried(
        volts, coef, jnp.exp(rate), 1.0 / weight, taps, early
    )
    return whitened_by(moment, spectra, high, low, early)


def solution(mesh):
    placed = (P(None, None, "chan", "tm"), P(), P("chan"))
    return jax.shard_map(
        per_device, mesh=mesh, in_specs=placed, out_specs=P("chan", None, "tm"), check_vma=False
    )
```
